32 devices in a mesh: grp: 8 (over z, y), inner: 4 (over x, core).
Axes of the slice: x: 2, y: 2, z: 4, core: 2. Of those that a mesh axis runs over, the one named last changes fastest.
Arguments:
- b_tensor: bfloat16 [10, 256, 3072], P(None, ('grp', 'inner')), may hold values from -0.59765625 to 0.59765625
- occ_energy: float32 [10], replicated, may hold values from -2 to -0.5
- vir_energy: float32 [3072], replicated, may hold values from 0.5 to 4
- left_list: int32 [3], replicated, may hold values from 0 to 9
- right_occ: int32 [1], replicated, may hold values from 0 to 9
Outputs:
- gamma_aux: float32 [10, 256, 3072], P(None, ('grp', 'inner'))
The draws below stay inside these ranges and needn't reach their ends.
Inputs may be any that keep to these rules, and one draw needn't show every extreme that they name: `left_list`: each entry is an occupied orbital of the window; a first orbital may equal the second, and first orbitals may repeat. `right_occ`: an occupied orbital of the window.
All inputs are finite; a program needn't handle non-finite values.
Results may differ from the reference program's by a relative error of at most 0.0023.
Values may be sent and summed in bfloat16 or wider, within the bound.
A program may use at most 128 MiB of HBM per device.

```python
import jax
import jax.numpy as jnp
from jax import lax

OCC_W = 10
NI = 3
V = 3072
AUX = 256
N_GRP = 8


def level_of(rng, dims, pieces, low, top_value):
    gain = 1.0
    for dim, parts in pieces:
        draws = jax.random.uniform(jax.random.fold_in(jax.random.fold_in(rng, 6), dim), (parts,), jnp.float32, low / len(pieces), top_value / len(pieces))
        gain = gain * jnp.repeat(jnp.exp(draws), dims[dim] // parts).reshape((-1,) + (1,) * (len(dims) - 1 - dim))
    return gain


def scatter_about(rng, shape, spread, most, cuts=(), dtype=jnp.bfloat16):
    entries = jax.random.normal(rng, shape, jnp.float32) * spread
    if len(cuts) > 0:
        entries = level_of(rng, shape, cuts, -0.22, 0.18) * entries
    return jnp.clip(entries, min=-most, max=most).astype(dtype)


def setup_inputs(seed: int = 0) -> dict:
    seeds = jax.random.split(jax.random.key(seed), 6)
    return {
        "b_tensor": scatter_about(seeds[0], (OCC_W, AUX, V), 0.1, 0.59765625, ((1, 32),)),
        "occ_energy": jnp.clip(jax.random.uniform(seeds[1], (OCC_W,), jnp.float32, -2.0, -0.5), -2.0, -0.5),
        "vir_energy": jnp.clip(jax.random.uniform(seeds[2], (V,), jnp.float32, 0.5, 4.0), 0.5, 4.0),
        "left_list": jax.random.randint(seeds[3], (NI,), 0, OCC_W).astype(jnp.int32),
        "right_occ": jax.random.randint(seeds[4], (1,), 0, OCC_W).astype(jnp.int32),
    }


def add_group(total, blocks):
    left, right = blocks
    partial_value = lax.dot_general(left, right, (((0,), (0,)), ((), ())), preferred_element_type=jnp.float32)
    return total + partial_value, None


def reference(b_tensor, occ_energy, vir_energy, left_list, right_occ):
    gamma_aux = jnp.zeros((OCC_W, AUX, V), jnp.float32)
    second_occ = right_occ[0].astype(jnp.int32)
    block_right = lax.dynamic_index_in_dim(b_tensor, second_occ, 0, keepdims=False)
    grouped_right = block_right.reshape(N_GRP, AUX // N_GRP, V)
    for pair_no in range(NI):
        left_occ = left_list[pair_no].astype(jnp.int32)
        block_left = lax.dynamic_index_in_dim(b_tensor, left_occ, 0, keepdims=False)
        grouped_left = block_left.reshape(N_GRP, AUX // N_GRP, V)
        integral, unused = lax.scan(add_group, jnp.zeros((V, V), jnp.float32), (grouped_left, grouped_right))
        shift_occ = occ_energy[left_occ] + occ_energy[second_occ]
        denominator = shift_occ - vir_energy[:, None] - vir_energy[None, :]
        amplitude = (integral / denominator).astype(jnp.bfloat16)
        contribution = lax.dot_general(block_right, amplitude, (((1,), (1,)), ((), ())), preferred_element_type=jnp.float32)
        gamma_aux = gamma_aux.at[left_occ].add(contribution)
    return gamma_aux
```

```python
import jax
import jax.numpy as jnp
from jax import lax
from jax.sharding import PartitionSpec as P


def body(b_tensor, occ_energy, vir_energy, left_list, right_occ):
    inner_size = lax.axis_size("inner")
    group_size = lax.axis_size("grp")
    occ_count = b_tensor.shape[0]
    virtuals = b_tensor.shape[2]
    row_count = virtuals // inner_size
    col_count = virtuals // group_size
    inner_rank = lax.axis_index("inner")
    group_rank = lax.axis_index("grp")
    vir_rows = lax.dynamic_slice_in_dim(vir_energy, inner_rank * row_count, row_count)
    vir_cols = lax.dynamic_slice_in_dim(vir_energy, group_rank * col_count, col_count)
    gamma_aux = jnp.zeros(b_tensor.shape, jnp.float32)
    orbitals = jnp.arange(occ_count, dtype=jnp.int32)
    second_occ = right_occ[0]
    block_right = lax.dynamic_index_in_dim(b_tensor, second_occ, 0, keepdims=False)
    right_full = lax.all_gather(block_right, "inner", axis=0, tiled=True)
    pair_total = left_list.shape[0]
    selectors = []
    shifts = []
    partials = []
    amp_list = []
    for pair_no in range(pair_total):
        left_occ = left_list[pair_no]
        block_left = lax.dynamic_index_in_dim(b_tensor, left_occ, 0, keepdims=False)
        left_rows = lax.all_to_all(block_left, "inner", split_axis=1, concat_axis=0, tiled=True)
        partial_value = lax.dot_general(
            left_rows, right_full, (((0,), (0,)), ((), ())), preferred_element_type=jnp.float32
        )
        shift_occ = occ_energy[left_occ] + occ_energy[second_occ]
        selectors.append((orbitals == left_occ).astype(jnp.float32))
        partials.append(partial_value)
        shifts.append(shift_occ)
    stacked = jnp.stack(partials, axis=0)
    shares_all = lax.psum_scatter(stacked, "grp", scatter_dimension=2, tiled=True)
    shift_all = jnp.stack(shifts, axis=0)
    denominator_all = shift_all[:, None, None] - vir_rows[None, :, None] - vir_cols[None, None, :]
    amp_tiles = (shares_all / denominator_all).astype(jnp.bfloat16)
    amp_whole = lax.all_gather(amp_tiles, "grp", axis=2, tiled=True)
    amp_list = [amp_whole[pair_no] for pair_no in range(pair_total)]
    for pair_no in range(pair_total):
        contrib = lax.dot_general(
            right_full,
            amp_list[pair_no],
            (((1,), (1,)), ((), ())),
            preferred_element_type=jnp.float32,
        )
        returned = lax.all_to_all(contrib, "inner", split_axis=0, concat_axis=1, tiled=True)
        gamma_aux = gamma_aux + selectors[pair_no][:, None, None] * returned[None]
    return gamma_aux


def body_rows(b_tensor, occ_energy, vir_energy, left_list, right_occ):
    axes = ("grp", "inner")
    devices = lax.axis_size("grp") * lax.axis_size("inner")
    me = lax.axis_index("grp") * lax.axis_size("inner") + lax.axis_index("inner")
    occ_count, aux_rows, virtuals = b_tensor.shape
    pair_total = left_list.shape[0]
    width = virtuals // devices
    second_occ = right_occ[0]
    block_right = lax.dynamic_index_in_dim(b_tensor, second_occ, 0, keepdims=False)
    block_left = jnp.take(b_tensor, left_list, axis=0)
    right_full = lax.all_gather(block_right, axes, axis=0, tiled=True)
    left_cols = lax.all_to_all(block_left, axes, split_axis=2, concat_axis=1, tiled=True)
    integral = lax.dot_general(
        left_cols, right_full, (((1,), (0,)), ((), ())), preferred_element_type=jnp.float32
    )
    vir_rows = lax.dynamic_slice_in_dim(vir_energy, me * width, width)
    shift = occ_energy[left_list] + occ_energy[second_occ]
    denominator = shift[:, None, None] - vir_rows[None, :, None] - vir_energy[None, None, :]
    amplitude = (integral / denominator).astype(jnp.bfloat16)
    contrib = lax.dot_general(
        amplitude, right_full, (((2,), (1,)), ((), ())), preferred_element_type=jnp.float32
    )
    returned = lax.all_to_all(contrib, axes, split_axis=2, concat_axis=1, tiled=True)
    returned = jnp.swapaxes(returned, 1, 2)
    selector = (jnp.arange(occ_count)[:, None] == left_list[None, :]).astype(jnp.float32)
    gamma_aux = jnp.zeros(b_tensor.shape, jnp.float32)
    for pair_no in range(pair_total):
        gamma_aux = gamma_aux + selector[:, pair_no][:, None, None] * returned[pair_no][None]
    return gamma_aux


GATHER_BYTES = 4 * 2**20


def solution(mesh):
    placed = (P(None, ("grp", "inner"), None), P(), P(), P(), P())

    def program(b_tensor, *rest):
        aux, virtuals = b_tensor.shape[1:]
        fits = 2 * aux * virtuals <= GATHER_BYTES and virtuals % mesh.size == 0
        return jax.shard_map(
            body_rows if fits else body,
            mesh=mesh,
            in_specs=placed,
            out_specs=P(None, ("grp", "inner"), None),
            check_vma=False,
        )(b_tensor, *rest)

    return program
```

```python
import jax
import jax.numpy as jnp
from jax import lax
from jax.experimental import pallas as pl
from jax.experimental.pallas import tpu as pltpu
from jax.sharding import PartitionSpec as P

MESH = pl.DeviceIdType.MESH
LANES = 128


def body(b_tensor, occ_energy, vir_energy, left_list, right_occ):
    inner_size = lax.axis_size("inner")
    group_size = lax.axis_size("grp")
    occ_count = b_tensor.shape[0]
    virtuals = b_tensor.shape[2]
    row_count = virtuals // inner_size
    col_count = virtuals // group_size
    inner_rank = lax.axis_index("inner")
    group_rank = lax.axis_index("grp")
    vir_rows = lax.dynamic_slice_in_dim(vir_energy, inner_rank * row_count, row_count)
    vir_cols = lax.dynamic_slice_in_dim(vir_energy, group_rank * col_count, col_count)
    gamma_aux = jnp.zeros(b_tensor.shape, jnp.float32)
    orbitals = jnp.arange(occ_count, dtype=jnp.int32)
    second_occ = right_occ[0]
    block_right = lax.dynamic_index_in_dim(b_tensor, second_occ, 0, keepdims=False)
    right_full = lax.all_gather(block_right, "inner", axis=0, tiled=True)
    pair_total = left_list.shape[0]
    selectors = []
    shifts = []
    partials = []
    amp_list = []
    for pair_no in range(pair_total):
        left_occ = left_list[pair_no]
        block_left = lax.dynamic_index_in_dim(b_tensor, left_occ, 0, keepdims=False)
        left_rows = lax.all_to_all(block_left, "inner", split_axis=1, concat_axis=0, tiled=True)
        partial_value = lax.dot_general(
            left_rows, right_full, (((0,), (0,)), ((), ())), preferred_element_type=jnp.float32
        )
        shift_occ = occ_energy[left_occ] + occ_energy[second_occ]
        selectors.append((orbitals == left_occ).astype(jnp.float32))
        partials.append(partial_value)
        shifts.append(shift_occ)
    stacked = jnp.stack(partials, axis=0)
    shares_all = lax.psum_scatter(stacked, "grp", scatter_dimension=2, tiled=True)
    shift_all = jnp.stack(shifts, axis=0)
    denominator_all = shift_all[:, None, None] - vir_rows[None, :, None] - vir_cols[None, None, :]
    amp_tiles = (shares_all / denominator_all).astype(jnp.bfloat16)
    amp_whole = lax.all_gather(amp_tiles, "grp", axis=2, tiled=True)
    amp_list = [amp_whole[pair_no] for pair_no in range(pair_total)]
    for pair_no in range(pair_total):
        contrib = lax.dot_general(
            right_full,
            amp_list[pair_no],
            (((1,), (1,)), ((), ())),
            preferred_element_type=jnp.float32,
        )
        returned = lax.all_to_all(contrib, "inner", split_axis=0, concat_axis=1, tiled=True)
        gamma_aux = gamma_aux + selectors[pair_no][:, None, None] * returned[None]
    return gamma_aux


def place(grp, inner):
    return grp // 2, grp % 2, inner // 2, inner % 2


def tile_owner(tile):
    grp = tile // 3
    slot = tile % 3
    idle = 2 * ((grp // 2 + grp % 2) % 2) + 1
    return grp, slot + jnp.where(slot >= idle, 1, 0)


def flip_z(z, step):
    return (z, z + 1 - 2 * (z % 2), (z + 2) % 4, 3 - z)[step]


def kernel(
    b_ref, occ_ref, vir_ref, left_ref, right_ref, out_ref,
    own, sib, pair_rows, full, left_cols, left_rows, contrib,
    swap_send, swap_recv, gather_send, gather_recv, left_send, left_recv, out_send, out_recv,
):
    grp, inner = lax.axis_index("grp"), lax.axis_index("inner")
    z, y, x, core = place(grp, inner)
    me = grp * 4 + inner
    chip = grp * 2 + x
    pairs = out_ref.shape[0]
    virtuals = full.shape[1]
    half = virtuals // 2
    quarter = virtuals // 4
    tiles = virtuals // LANES

    barrier = pltpu.get_barrier_semaphore()

    @pl.loop(1, 32)
    def _(step):
        other = (me + step) % 32
        pl.semaphore_signal(barrier, inc=1, device_id=(other // 4, other % 4), device_id_type=MESH)

    second = right_ref[0]
    own[pl.ds(0, 8), :] = b_ref[second]
    for pair in range(pairs):
        own[pl.ds(8 * pair + 8, 8), :] = b_ref[left_ref[pair]]
    pl.semaphore_wait(barrier, 31)

    sibling = (grp, inner + 1 - 2 * core)
    swap = pltpu.make_async_remote_copy(
        src_ref=own, dst_ref=sib, send_sem=swap_send, recv_sem=swap_recv, device_id=sibling, device_id_type=MESH
    )
    swap.start()
    swap.wait_recv()

    def merge(low, high):
        for block in range(pairs + 1):
            pair_rows[block, pl.ds(0, 8), :] = low[pl.ds(8 * block, 8), :]
            pair_rows[block, pl.ds(8, 8), :] = high[pl.ds(8 * block, 8), :]

    @pl.when(core == 0)
    def _():
        merge(own, sib)

    @pl.when(core == 1)
    def _():
        merge(sib, own)

    full[pl.ds(pl.multiple_of(chip * 16, 16), 16), :] = pair_rows[0]

    my_col = core * half
    x_side = (grp, (1 - x) * 2 + core)
    y_side = (z * 2 + 1 - y, inner)
    started = []

    def send(slot, z_of, y_of, x_of, first, count, target):
        row = pl.multiple_of(((z_of * 2 + y_of) * 2 + x_of) * 16, 16)
        piece = full.at[pl.ds(row, 16), pl.ds(pl.multiple_of(first, LANES), count)]
        copy = pltpu.make_async_remote_copy(
            src_ref=piece, dst_ref=piece, send_sem=gather_send.at[slot], recv_sem=gather_recv.at[slot],
            device_id=target, device_id_type=MESH,
        )
        copy.start()
        started.append(copy)

    def arrived(slot, z_of, y_of, x_of, first, count):
        row = pl.multiple_of(((z_of * 2 + y_of) * 2 + x_of) * 16, 16)
        piece = full.at[pl.ds(row, 16), pl.ds(pl.multiple_of(first, LANES), count)]
        pltpu.make_async_remote_copy(
            src_ref=piece, dst_ref=piece, send_sem=gather_send.at[slot], recv_sem=gather_recv.at[slot],
            device_id=sibling, device_id_type=MESH,
        ).wait_recv()

    Z, X1, Y1, X2, Y2, CZ, CX, CY, CD = 0, 4, 8, 12, 16, 20, 24, 28, 32

    def spread(step):
        z_of = flip_z(z, step)
        send(X1 + step, z_of, y, x, my_col, half, x_side)
        send(Y1 + step, z_of, y, x, my_col, half, y_side)

    for step in (1, 2, 3):
        send(Z + step, z, y, x, my_col, half, (flip_z(z, step) * 2 + y, inner))
    spread(0)

    chip_rows = pl.ds(pl.multiple_of(chip * 16, 16), 16)

    def left_copy(index):
        tile = 2 * index + core
        to_grp, to_inner = tile_owner(tile)
        copy = pltpu.make_async_remote_copy(
            src_ref=pair_rows.at[pl.ds(1, pairs), :, pl.ds(pl.multiple_of(tile * LANES, LANES), LANES)],
            dst_ref=left_cols.at[:, chip_rows, :],
            send_sem=left_send.at[index],
            recv_sem=left_recv.at[chip],
            device_id=(to_grp, to_inner),
            device_id_type=MESH,
        )
        return to_grp * 2 + to_inner // 2 != chip, copy

    @pl.loop(0, tiles // 2)
    def _(step):
        index = (step + 3 * (grp // 2)) % (tiles // 2)
        away, copy = left_copy(index)

        @pl.when(away)
        def _():
            copy.start()

    def relay(step):
        z_of = flip_z(z, step)
        arrived(X1 + step, z_of, y, 1 - x, my_col, half)
        send(Y2 + step, z_of, y, 1 - x, my_col, quarter, y_side)
        send(CX + step, z_of, y, 1 - x, my_col, half, sibling)
        arrived(Y1 + step, z_of, 1 - y, x, my_col, half)
        send(X2 + step, z_of, 1 - y, x, my_col + quarter, quarter, x_side)
        send(CY + step, z_of, 1 - y, x, my_col, half, sibling)

    def finish(step):
        z_of = flip_z(z, step)
        arrived(Y2 + step, z_of, 1 - y, 1 - x, my_col, quarter)
        arrived(X2 + step, z_of, 1 - y, 1 - x, my_col + quarter, quarter)
        send(CD + step, z_of, 1 - y, 1 - x, my_col, half, sibling)

    for step in (1, 2, 3):
        z_of = flip_z(z, step)
        arrived(Z + step, z_of, y, x, my_col, half)
        spread(step)
        send(CZ + step, z_of, y, x, my_col, half, sibling)
        relay(step - 1)
        if step > 1:
            finish(step - 2)
    relay(3)
    finish(2)
    finish(3)
    other_col = (1 - core) * half
    for step in range(4):
        z_of = flip_z(z, step)
        if step:
            arrived(CZ + step, z_of, y, x, other_col, half)
        arrived(CX + step, z_of, y, 1 - x, other_col, half)
        arrived(CY + step, z_of, 1 - y, x, other_col, half)
        arrived(CD + step, z_of, 1 - y, 1 - x, other_col, half)

    idle = 2 * ((z + y) % 2) + 1
    my_tile = grp * 3 + inner - jnp.where(inner > idle, 1, 0)
    my_lanes = pl.ds(pl.multiple_of(my_tile * LANES, LANES), LANES)

    def out_copy(step):
        other = (me + step) % 32
        return pltpu.make_async_remote_copy(
            src_ref=contrib.at[:, pl.ds(pl.multiple_of(other * 8, 8), 8), :],
            dst_ref=out_ref.at[:, :, my_lanes],
            send_sem=out_send.at[step],
            recv_sem=out_recv.at[my_tile],
            device_id=(other // 4, other % 4),
            device_id_type=MESH,
        )

    @pl.when(inner != idle)
    def _():
        left_cols[:, chip_rows, :] = pair_rows[pl.ds(1, pairs), :, my_lanes]

        @pl.loop(1, 16)
        def _(step):
            source = (chip + step) % 16
            pltpu.make_async_remote_copy(
                src_ref=pair_rows.at[pl.ds(1, pairs), :, pl.ds(0, LANES)],
                dst_ref=left_cols.at[:, pl.ds(pl.multiple_of(source * 16, 16), 16), :],
                send_sem=left_send.at[0],
                recv_sem=left_recv.at[source],
                device_id=sibling,
                device_id_type=MESH,
            ).wait_recv()

        vir_cols = jnp.transpose(jnp.broadcast_to(vir_ref[:, my_lanes], (LANES, LANES)))[:, :1]
        shifts = []
        for pair in range(pairs):
            left_rows[pl.ds(pair * LANES, LANES), :] = jnp.transpose(left_cols[pair])
            shifts.append((occ_ref[left_ref[pair]] + occ_ref[second]) - vir_cols)
        shift = jnp.concatenate(shifts, axis=0)
        contrib[...] = jnp.zeros_like(contrib)
        wide = 4 * LANES

        @pl.loop(0, virtuals // wide)
        def _(part):
            columns = pl.ds(pl.multiple_of(part * wide, wide), wide)
            block = full[:, columns]
            integral = jnp.dot(left_rows[...], block, preferred_element_type=jnp.float32)
            amplitude = (integral / (shift - vir_ref[:, columns])).astype(jnp.bfloat16)
            for pair in range(pairs):
                contrib[pair] += lax.dot_general(
                    block, amplitude[pair * LANES : (pair + 1) * LANES], (((1,), (1,)), ((), ())),
                    preferred_element_type=jnp.float32,
                )

        out_ref[:, :, my_lanes] = contrib[:, pl.ds(pl.multiple_of(me * 8, 8), 8), :]

        @pl.loop(1, 32)
        def _(step):
            out_copy(step).start()

    swap.wait_send()
    for copy in started:
        copy.wait_send()

    @pl.loop(0, tiles // 2)
    def _(index):
        away, copy = left_copy(index)

        @pl.when(away)
        def _():
            copy.wait_send()

    @pl.loop(0, tiles)
    def _(tile):
        from_grp, from_inner = tile_owner(tile)

        @pl.when(from_grp * 4 + from_inner != me)
        def _():
            pltpu.make_async_remote_copy(
                src_ref=contrib.at[:, pl.ds(0, 8), :],
                dst_ref=out_ref.at[:, :, pl.ds(pl.multiple_of(tile * LANES, LANES), LANES)],
                send_sem=out_send.at[0],
                recv_sem=out_recv.at[tile],
                device_id=sibling,
                device_id_type=MESH,
            ).wait_recv()

    @pl.when(inner != idle)
    def _():
        @pl.loop(1, 32)
        def _(step):
            out_copy(step).wait_send()


def body_tiles(b_tensor, occ_energy, vir_energy, left_list, right_occ):
    occ_count, aux_rows, virtuals = b_tensor.shape
    pairs = left_list.shape[0]
    aux = 32 * aux_rows
    vmem, smem = pl.BlockSpec(memory_space=pltpu.VMEM), pl.BlockSpec(memory_space=pltpu.SMEM)
    dma = pltpu.SemaphoreType.DMA
    returned = pl.pallas_call(
        kernel,
        out_shape=jax.ShapeDtypeStruct((pairs, aux_rows, virtuals), jnp.float32),
        in_specs=[vmem, smem, vmem, smem, smem],
        out_specs=vmem,
        scratch_shapes=[
            pltpu.VMEM(((pairs + 1) * aux_rows, virtuals), jnp.bfloat16),
            pltpu.VMEM(((pairs + 1) * aux_rows, virtuals), jnp.bfloat16),
            pltpu.VMEM((pairs + 1, 2 * aux_rows, virtuals), jnp.bfloat16),
            pltpu.VMEM((aux, virtuals), jnp.bfloat16),
            pltpu.VMEM((pairs, aux, LANES), jnp.bfloat16),
            pltpu.VMEM((pairs * LANES, aux), jnp.bfloat16),
            pltpu.VMEM((pairs, aux, LANES), jnp.float32),
            dma, dma, dma((36,)), dma((36,)), dma((virtuals // LANES,)), dma((16,)),
            dma((32,)), dma((virtuals // LANES,)),
        ],
        compiler_params=pltpu.CompilerParams(
            collective_id=0, has_side_effects=True, vmem_limit_bytes=32 * 2**20
        ),
        cost_estimate=pl.CostEstimate(
            flops=4 * pairs * aux * virtuals * LANES, bytes_accessed=2 * occ_count * aux_rows * virtuals, transcendentals=0
        ),
    )(b_tensor, occ_energy, vir_energy.reshape(1, virtuals), left_list, right_occ)
    selector = (jnp.arange(occ_count)[:, None] == left_list[None, :]).astype(jnp.float32)
    gamma_aux = jnp.zeros(b_tensor.shape, jnp.float32)
    for pair_no in range(pairs):
        gamma_aux = gamma_aux + selector[:, pair_no][:, None, None] * returned[pair_no][None]
    return gamma_aux


def solution(mesh):
    placed = (P(None, ("grp", "inner"), None), P(), P(), P(), P())
    plan = body
    if mesh.shape["grp"] == 8 and mesh.shape["inner"] == 4:
        plan = body_tiles

    def program(b_tensor, *rest):
        aux, virtuals = b_tensor.shape[1:]
        fits = aux == 256 and virtuals == 3072
        return jax.shard_map(
            plan if fits else body,
            mesh=mesh,
            in_specs=placed,
            out_specs=P(None, ("grp", "inner"), None),
            check_vma=False,
        )(b_tensor, *rest)

    return program
```

```python
import jax
import jax.numpy as jnp
from jax import lax
from jax.experimental import pallas as pl
from jax.experimental.pallas import tpu as pltpu
from jax.sharding import PartitionSpec as P

MESH = pl.DeviceIdType.MESH
LANES = 128


def body(b_tensor, occ_energy, vir_energy, left_list, right_occ):
    inner_size = lax.axis_size("inner")
    group_size = lax.axis_size("grp")
    occ_count = b_tensor.shape[0]
    virtuals = b_tensor.shape[2]
    row_count = virtuals // inner_size
    col_count = virtuals // group_size
    inner_rank = lax.axis_index("inner")
    group_rank = lax.axis_index("grp")
    vir_rows = lax.dynamic_slice_in_dim(vir_energy, inner_rank * row_count, row_count)
    vir_cols = lax.dynamic_slice_in_dim(vir_energy, group_rank * col_count, col_count)
    gamma_aux = jnp.zeros(b_tensor.shape, jnp.float32)
    orbitals = jnp.arange(occ_count, dtype=jnp.int32)
    second_occ = right_occ[0]
    block_right = lax.dynamic_index_in_dim(b_tensor, second_occ, 0, keepdims=False)
    right_full = lax.all_gather(block_right, "inner", axis=0, tiled=True)
    pair_total = left_list.shape[0]
    selectors = []
    shifts = []
    partials = []
    amp_list = []
    for pair_no in range(pair_total):
        left_occ = left_list[pair_no]
        block_left = lax.dynamic_index_in_dim(b_tensor, left_occ, 0, keepdims=False)
        left_rows = lax.all_to_all(block_left, "inner", split_axis=1, concat_axis=0, tiled=True)
        partial_value = lax.dot_general(
            left_rows, right_full, (((0,), (0,)), ((), ())), preferred_element_type=jnp.float32
        )
        shift_occ = occ_energy[left_occ] + occ_energy[second_occ]
        selectors.append((orbitals == left_occ).astype(jnp.float32))
        partials.append(partial_value)
        shifts.append(shift_occ)
    stacked = jnp.stack(partials, axis=0)
    shares_all = lax.psum_scatter(stacked, "grp", scatter_dimension=2, tiled=True)
    shift_all = jnp.stack(shifts, axis=0)
    denominator_all = shift_all[:, None, None] - vir_rows[None, :, None] - vir_cols[None, None, :]
    amp_tiles = (shares_all / denominator_all).astype(jnp.bfloat16)
    amp_whole = lax.all_gather(amp_tiles, "grp", axis=2, tiled=True)
    amp_list = [amp_whole[pair_no] for pair_no in range(pair_total)]
    for pair_no in range(pair_total):
        contrib = lax.dot_general(
            right_full,
            amp_list[pair_no],
            (((1,), (1,)), ((), ())),
            preferred_element_type=jnp.float32,
        )
        returned = lax.all_to_all(contrib, "inner", split_axis=0, concat_axis=1, tiled=True)
        gamma_aux = gamma_aux + selectors[pair_no][:, None, None] * returned[None]
    return gamma_aux


def place(grp, inner):
    return grp // 2, grp % 2, inner // 2, inner % 2


def tile_owner(tile):
    grp = tile // 3
    slot = tile % 3
    idle = 2 * ((grp // 2 + grp % 2) % 2) + 1
    return grp, slot + jnp.where(slot >= idle, 1, 0)


def flip_z(z, step):
    return (z, z + 1 - 2 * (z % 2), (z + 2) % 4, 3 - z)[step]


def kernel(
    b_hbm, occ_hbm, vir_hbm, left_hbm, right_hbm, gamma_ref,
    b_ref, occ_ref, vir_ref, left_ref, right_ref, input_sem, out_ref, own, sib, pair_rows, full, left_cols, left_rows, contrib,
    swap_send, swap_recv, gather_send, gather_recv, left_send, left_recv, out_send, out_recv,
):
    grp, inner = lax.axis_index("grp"), lax.axis_index("inner")
    z, y, x, core = place(grp, inner)
    me = grp * 4 + inner
    chip = grp * 2 + x
    pairs = out_ref.shape[0]
    virtuals = full.shape[1]
    half = virtuals // 2
    quarter = virtuals // 4
    tiles = virtuals // LANES

    inputs = ((b_hbm, b_ref), (occ_hbm, occ_ref), (vir_hbm, vir_ref), (left_hbm, left_ref), (right_hbm, right_ref))
    fetches = [pltpu.make_async_copy(a, b, input_sem.at[n]) for n, (a, b) in enumerate(inputs)]
    for fetch in fetches:
        fetch.start()
    barrier = pltpu.get_barrier_semaphore()

    @pl.loop(1, 32)
    def _(step):
        other = (me + step) % 32
        pl.semaphore_signal(barrier, inc=1, device_id=(other // 4, other % 4), device_id_type=MESH)

    for fetch in fetches:
        fetch.wait()
    second = right_ref[0]
    own[pl.ds(0, 8), :] = b_ref[second]
    for pair in range(pairs):
        own[pl.ds(8 * pair + 8, 8), :] = b_ref[left_ref[pair]]
    pl.semaphore_wait(barrier, 31)

    sibling = (grp, inner + 1 - 2 * core)
    swap = pltpu.make_async_remote_copy(
        src_ref=own, dst_ref=sib, send_sem=swap_send, recv_sem=swap_recv, device_id=sibling, device_id_type=MESH
    )
    swap.start()
    swap.wait_recv()

    def merge(low, high):
        for block in range(pairs + 1):
            pair_rows[block, pl.ds(0, 8), :] = low[pl.ds(8 * block, 8), :]
            pair_rows[block, pl.ds(8, 8), :] = high[pl.ds(8 * block, 8), :]

    @pl.when(core == 0)
    def _():
        merge(own, sib)

    @pl.when(core == 1)
    def _():
        merge(sib, own)

    full[pl.ds(pl.multiple_of(chip * 16, 16), 16), :] = pair_rows[0]

    my_col = core * half
    x_side = (grp, (1 - x) * 2 + core)
    y_side = (z * 2 + 1 - y, inner)
    started = []

    def send(slot, z_of, y_of, x_of, first, count, target):
        row = pl.multiple_of(((z_of * 2 + y_of) * 2 + x_of) * 16, 16)
        piece = full.at[pl.ds(row, 16), pl.ds(pl.multiple_of(first, LANES), count)]
        copy = pltpu.make_async_remote_copy(
            src_ref=piece, dst_ref=piece, send_sem=gather_send.at[slot], recv_sem=gather_recv.at[slot],
            device_id=target, device_id_type=MESH,
        )
        copy.start()
        started.append(copy)

    def arrived(slot, z_of, y_of, x_of, first, count):
        row = pl.multiple_of(((z_of * 2 + y_of) * 2 + x_of) * 16, 16)
        piece = full.at[pl.ds(row, 16), pl.ds(pl.multiple_of(first, LANES), count)]
        pltpu.make_async_remote_copy(
            src_ref=piece, dst_ref=piece, send_sem=gather_send.at[slot], recv_sem=gather_recv.at[slot],
            device_id=sibling, device_id_type=MESH,
        ).wait_recv()

    Z, X1, Y1, X2, Y2, CZ, CX, CY, CD = 0, 4, 8, 12, 16, 20, 24, 28, 32

    def spread(step):
        z_of = flip_z(z, step)
        send(X1 + step, z_of, y, x, my_col, half, x_side)
        send(Y1 + step, z_of, y, x, my_col, half, y_side)

    for step in (1, 2, 3):
        send(Z + step, z, y, x, my_col, half, (flip_z(z, step) * 2 + y, inner))
    spread(0)

    chip_rows = pl.ds(pl.multiple_of(chip * 16, 16), 16)

    def left_copy(index):
        tile = 2 * index + core
        to_grp, to_inner = tile_owner(tile)
        copy = pltpu.make_async_remote_copy(
            src_ref=pair_rows.at[pl.ds(1, pairs), :, pl.ds(pl.multiple_of(tile * LANES, LANES), LANES)],
            dst_ref=left_cols.at[:, chip_rows, :],
            send_sem=left_send.at[index],
            recv_sem=left_recv.at[chip],
            device_id=(to_grp, to_inner),
            device_id_type=MESH,
        )
        return to_grp * 2 + to_inner // 2 != chip, copy

    @pl.loop(0, tiles // 2)
    def _(step):
        index = (step + 3 * (grp // 2)) % (tiles // 2)
        away, copy = left_copy(index)

        @pl.when(away)
        def _():
            copy.start()

    def relay(step):
        z_of = flip_z(z, step)
        arrived(X1 + step, z_of, y, 1 - x, my_col, half)
        send(Y2 + step, z_of, y, 1 - x, my_col, quarter, y_side)
        send(CX + step, z_of, y, 1 - x, my_col, half, sibling)
        arrived(Y1 + step, z_of, 1 - y, x, my_col, half)
        send(X2 + step, z_of, 1 - y, x, my_col + quarter, quarter, x_side)
        send(CY + step, z_of, 1 - y, x, my_col, half, sibling)

    def finish(step):
        z_of = flip_z(z, step)
        arrived(Y2 + step, z_of, 1 - y, 1 - x, my_col, quarter)
        arrived(X2 + step, z_of, 1 - y, 1 - x, my_col + quarter, quarter)
        send(CD + step, z_of, 1 - y, 1 - x, my_col, half, sibling)

    for step in (1, 2, 3):
        z_of = flip_z(z, step)
        arrived(Z + step, z_of, y, x, my_col, half)
        spread(step)
        send(CZ + step, z_of, y, x, my_col, half, sibling)
        relay(step - 1)
        if step > 1:
            finish(step - 2)
    relay(3)
    finish(2)
    finish(3)
    other_col = (1 - core) * half
    for step in range(4):
        z_of = flip_z(z, step)
        if step:
            arrived(CZ + step, z_of, y, x, other_col, half)
        arrived(CX + step, z_of, y, 1 - x, other_col, half)
        arrived(CY + step, z_of, 1 - y, x, other_col, half)
        arrived(CD + step, z_of, 1 - y, 1 - x, other_col, half)

    idle = 2 * ((z + y) % 2) + 1
    my_tile = grp * 3 + inner - jnp.where(inner > idle, 1, 0)
    my_lanes = pl.ds(pl.multiple_of(my_tile * LANES, LANES), LANES)

    def out_copy(step):
        other = (me + step) % 32
        return pltpu.make_async_remote_copy(
            src_ref=contrib.at[:, pl.ds(pl.multiple_of(other * 8, 8), 8), :],
            dst_ref=out_ref.at[:, :, my_lanes],
            send_sem=out_send.at[step],
            recv_sem=out_recv.at[my_tile],
            device_id=(other // 4, other % 4),
            device_id_type=MESH,
        )

    @pl.when(inner != idle)
    def _():
        left_cols[:, chip_rows, :] = pair_rows[pl.ds(1, pairs), :, my_lanes]

        @pl.loop(1, 16)
        def _(step):
            source = (chip + step) % 16
            pltpu.make_async_remote_copy(
                src_ref=pair_rows.at[pl.ds(1, pairs), :, pl.ds(0, LANES)],
                dst_ref=left_cols.at[:, pl.ds(pl.multiple_of(source * 16, 16), 16), :],
                send_sem=left_send.at[0],
                recv_sem=left_recv.at[source],
                device_id=sibling,
                device_id_type=MESH,
            ).wait_recv()

        vir_cols = jnp.transpose(jnp.broadcast_to(vir_ref[:, my_lanes], (LANES, LANES)))[:, :1]
        shifts = []
        for pair in range(pairs):
            left_rows[pl.ds(pair * LANES, LANES), :] = jnp.transpose(left_cols[pair])
            shifts.append((occ_ref[left_ref[pair]] + occ_ref[second]) - vir_cols)
        shift = jnp.concatenate(shifts, axis=0)
        wide = 4 * LANES
        total = jnp.zeros((pairs * LANES, full.shape[0]), jnp.float32)
        for part in range(virtuals // wide):
            columns = pl.ds(part * wide, wide)
            block = full[:, columns]
            integral = jnp.dot(left_rows[...], block, preferred_element_type=jnp.float32)
            denominator = shift - vir_ref[:, columns]
            inverse = pl.reciprocal(denominator, approx=True)
            inverse = inverse * (2.0 - denominator * inverse)
            amplitude = (integral * inverse).astype(jnp.bfloat16)
            total += lax.dot_general(
                amplitude, block, (((1,), (1,)), ((), ())), preferred_element_type=jnp.float32
            )
        for pair in range(pairs):
            contrib[pair] = jnp.transpose(total[pair * LANES : (pair + 1) * LANES])

        out_ref[:, :, my_lanes] = contrib[:, pl.ds(pl.multiple_of(me * 8, 8), 8), :]

        @pl.loop(1, 32)
        def _(step):
            out_copy(step).start()

    swap.wait_send()
    for copy in started:
        copy.wait_send()

    @pl.loop(0, tiles // 2)
    def _(index):
        away, copy = left_copy(index)

        @pl.when(away)
        def _():
            copy.wait_send()

    @pl.loop(0, tiles)
    def _(tile):
        from_grp, from_inner = tile_owner(tile)

        @pl.when(from_grp * 4 + from_inner != me)
        def _():
            pltpu.make_async_remote_copy(
                src_ref=contrib.at[:, pl.ds(0, 8), :],
                dst_ref=out_ref.at[:, :, pl.ds(pl.multiple_of(tile * LANES, LANES), LANES)],
                send_sem=out_send.at[0],
                recv_sem=out_recv.at[tile],
                device_id=sibling,
                device_id_type=MESH,
            ).wait_recv()

    for orbital in range(gamma_ref.shape[0]):
        row = jnp.where(left_ref[0] == orbital, out_ref[0], 0.0)
        for pair in range(1, pairs):
            row += jnp.where(left_ref[pair] == orbital, out_ref[pair], 0.0)
        gamma_ref[orbital] = row

    @pl.when(inner != idle)
    def _():
        @pl.loop(1, 32)
        def _(step):
            out_copy(step).wait_send()


def body_tiles(b_tensor, occ_energy, vir_energy, left_list, right_occ):
    occ_count, aux_rows, virtuals = b_tensor.shape
    pairs = left_list.shape[0]
    aux = 32 * aux_rows
    hbm, vmem = pl.BlockSpec(memory_space=pltpu.HBM), pl.BlockSpec(memory_space=pltpu.VMEM)
    dma = pltpu.SemaphoreType.DMA
    return pl.pallas_call(
        kernel,
        out_shape=jax.ShapeDtypeStruct(b_tensor.shape, jnp.float32),
        in_specs=[hbm] * 5,
        out_specs=vmem,
        scratch_shapes=[
            pltpu.VMEM(b_tensor.shape, jnp.bfloat16),
            pltpu.SMEM(occ_energy.shape, jnp.float32),
            pltpu.VMEM((1, virtuals), jnp.float32),
            pltpu.SMEM(left_list.shape, jnp.int32),
            pltpu.SMEM(right_occ.shape, jnp.int32),
            dma((5,)),
            pltpu.VMEM((pairs, aux_rows, virtuals), jnp.float32),
            pltpu.VMEM(((pairs + 1) * aux_rows, virtuals), jnp.bfloat16),
            pltpu.VMEM(((pairs + 1) * aux_rows, virtuals), jnp.bfloat16),
            pltpu.VMEM((pairs + 1, 2 * aux_rows, virtuals), jnp.bfloat16),
            pltpu.VMEM((aux, virtuals), jnp.bfloat16),
            pltpu.VMEM((pairs, aux, LANES), jnp.bfloat16),
            pltpu.VMEM((pairs * LANES, aux), jnp.bfloat16),
            pltpu.VMEM((pairs, aux, LANES), jnp.float32),
            dma, dma, dma((36,)), dma((36,)), dma((virtuals // LANES,)), dma((16,)),
            dma((32,)), dma((virtuals // LANES,)),
        ],
        compiler_params=pltpu.CompilerParams(
            collective_id=0, has_side_effects=True, vmem_limit_bytes=60 * 2**20
        ),
        cost_estimate=pl.CostEstimate(
            flops=4 * pairs * aux * virtuals * LANES, bytes_accessed=2 * occ_count * aux_rows * virtuals, transcendentals=0
        ),
    )(b_tensor, occ_energy, vir_energy.reshape(1, virtuals), left_list, right_occ)


def solution(mesh):
    placed = (P(None, ("grp", "inner"), None), P(), P(), P(), P())
    plan = body
    if mesh.shape["grp"] == 8 and mesh.shape["inner"] == 4:
        plan = body_tiles

    def program(b_tensor, *rest):
        aux, virtuals = b_tensor.shape[1:]
        fits = aux == 256 and virtuals == 3072
        return jax.shard_map(
            plan if fits else body,
            mesh=mesh,
            in_specs=placed,
            out_specs=P(None, ("grp", "inner"), None),
            check_vma=False,
        )(b_tensor, *rest)

    return program
```

```python
import jax
import jax.numpy as jnp
from jax import lax
from jax.experimental import pallas as pl
from jax.experimental.pallas import tpu as pltpu
from jax.sharding import PartitionSpec as P

MESH = pl.DeviceIdType.MESH
LANES = 128


def body(b_tensor, occ_energy, vir_energy, left_list, right_occ):
    inner_size = lax.axis_size("inner")
    group_size = lax.axis_size("grp")
    occ_count = b_tensor.shape[0]
    virtuals = b_tensor.shape[2]
    row_count = virtuals // inner_size
    col_count = virtuals // group_size
    inner_rank = lax.axis_index("inner")
    group_rank = lax.axis_index("grp")
    vir_rows = lax.dynamic_slice_in_dim(vir_energy, inner_rank * row_count, row_count)
    vir_cols = lax.dynamic_slice_in_dim(vir_energy, group_rank * col_count, col_count)
    gamma_aux = jnp.zeros(b_tensor.shape, jnp.float32)
    orbitals = jnp.arange(occ_count, dtype=jnp.int32)
    second_occ = right_occ[0]
    block_right = lax.dynamic_index_in_dim(b_tensor, second_occ, 0, keepdims=False)
    right_full = lax.all_gather(block_right, "inner", axis=0, tiled=True)
    pair_total = left_list.shape[0]
    selectors = []
    shifts = []
    partials = []
    amp_list = []
    for pair_no in range(pair_total):
        left_occ = left_list[pair_no]
        block_left = lax.dynamic_index_in_dim(b_tensor, left_occ, 0, keepdims=False)
        left_rows = lax.all_to_all(block_left, "inner", split_axis=1, concat_axis=0, tiled=True)
        partial_value = lax.dot_general(
            left_rows, right_full, (((0,), (0,)), ((), ())), preferred_element_type=jnp.float32
        )
        shift_occ = occ_energy[left_occ] + occ_energy[second_occ]
        selectors.append((orbitals == left_occ).astype(jnp.float32))
        partials.append(partial_value)
        shifts.append(shift_occ)
    stacked = jnp.stack(partials, axis=0)
    shares_all = lax.psum_scatter(stacked, "grp", scatter_dimension=2, tiled=True)
    shift_all = jnp.stack(shifts, axis=0)
    denominator_all = shift_all[:, None, None] - vir_rows[None, :, None] - vir_cols[None, None, :]
    amp_tiles = (shares_all / denominator_all).astype(jnp.bfloat16)
    amp_whole = lax.all_gather(amp_tiles, "grp", axis=2, tiled=True)
    amp_list = [amp_whole[pair_no] for pair_no in range(pair_total)]
    for pair_no in range(pair_total):
        contrib = lax.dot_general(
            right_full,
            amp_list[pair_no],
            (((1,), (1,)), ((), ())),
            preferred_element_type=jnp.float32,
        )
        returned = lax.all_to_all(contrib, "inner", split_axis=0, concat_axis=1, tiled=True)
        gamma_aux = gamma_aux + selectors[pair_no][:, None, None] * returned[None]
    return gamma_aux


def place(grp, inner):
    return grp // 2, grp % 2, inner // 2, inner % 2


def tile_owner(tile):
    grp = tile // 3
    slot = tile % 3
    idle = 2 * ((grp // 2 + grp % 2) % 2) + 1
    return grp, slot + jnp.where(slot >= idle, 1, 0)


def flip_z(z, step):
    return (z, z + 1 - 2 * (z % 2), (z + 2) % 4, 3 - z)[step]


def kernel(
    b_hbm, occ_hbm, vir_hbm, left_hbm, right_hbm, out_ref,
    b_ref, occ_ref, vir_ref, left_ref, right_ref, input_sem, own, sib, folded, pair_rows, full, left_cols, left_rows, contrib,
    swap_send, swap_recv, gather_send, gather_recv, left_send, left_recv, out_send, out_recv,
):
    grp, inner = lax.axis_index("grp"), lax.axis_index("inner")
    z, y, x, core = place(grp, inner)
    me = grp * 4 + inner
    chip = grp * 2 + x
    pairs = out_ref.shape[0]
    half = full.shape[2]
    virtuals = 2 * half
    quarter = half // 2
    tiles = virtuals // LANES

    inputs = ((b_hbm, b_ref), (occ_hbm, occ_ref), (vir_hbm, vir_ref), (left_hbm, left_ref), (right_hbm, right_ref))
    fetches = [pltpu.make_async_copy(a, b, input_sem.at[n]) for n, (a, b) in enumerate(inputs)]
    for fetch in fetches:
        fetch.start()
    barrier = pltpu.get_barrier_semaphore()

    @pl.loop(1, 32)
    def _(step):
        other = (me + step) % 32
        pl.semaphore_signal(barrier, inc=1, device_id=(other // 4, other % 4), device_id_type=MESH)

    for fetch in fetches:
        fetch.wait()
    second = right_ref[0]
    folded[pl.ds(0, 8), :] = b_ref[second, :, pl.ds(0, half)]
    folded[pl.ds(8, 8), :] = b_ref[second, :, pl.ds(half, half)]
    full[me] = folded[...]
    own[pl.ds(0, 8), :] = b_ref[second]
    for pair in range(pairs):
        own[pl.ds(8 * pair + 8, 8), :] = b_ref[left_ref[pair]]
    pl.semaphore_wait(barrier, 31)

    sibling = (grp, inner + 1 - 2 * core)
    swap = pltpu.make_async_remote_copy(
        src_ref=own, dst_ref=sib, send_sem=swap_send, recv_sem=swap_recv, device_id=sibling, device_id_type=MESH
    )

    x_side = (grp, (1 - x) * 2 + core)
    y_side = (z * 2 + 1 - y, inner)
    started = []

    def send(slot, z_of, y_of, x_of, first, count, target):
        piece = full.at[(z_of * 2 + y_of) * 4 + x_of * 2 + core, :, pl.ds(first, count)]
        copy = pltpu.make_async_remote_copy(
            src_ref=piece, dst_ref=piece, send_sem=gather_send.at[slot], recv_sem=gather_recv.at[slot],
            device_id=target, device_id_type=MESH,
        )
        copy.start()
        started.append(copy)

    def arrived(slot, z_of, y_of, x_of, first, count, side=core):
        piece = full.at[(z_of * 2 + y_of) * 4 + x_of * 2 + side, :, pl.ds(first, count)]
        pltpu.make_async_remote_copy(
            src_ref=piece, dst_ref=piece, send_sem=gather_send.at[slot], recv_sem=gather_recv.at[slot],
            device_id=sibling, device_id_type=MESH,
        ).wait_recv()

    Z, X1, Y1, X2, Y2, CZ, CX, CY, CD = 0, 4, 8, 12, 16, 20, 24, 28, 32

    def spread(step):
        z_of = flip_z(z, step)
        send(X1 + step, z_of, y, x, 0, half, x_side)
        send(Y1 + step, z_of, y, x, 0, half, y_side)

    for step in (1, 2, 3):
        send(Z + step, z, y, x, 0, half, (flip_z(z, step) * 2 + y, inner))
    spread(0)
    send(CZ, z, y, x, 0, half, sibling)
    swap.start()

    def merge(low, high):
        for block in range(pairs):
            pair_rows[block, pl.ds(0, 8), :] = low[pl.ds(8 * block + 8, 8), :]
            pair_rows[block, pl.ds(8, 8), :] = high[pl.ds(8 * block + 8, 8), :]

    chip_rows = pl.ds(pl.multiple_of(chip * 16, 16), 16)

    def left_copy(index):
        tile = 2 * index + core
        to_grp, to_inner = tile_owner(tile)
        copy = pltpu.make_async_remote_copy(
            src_ref=pair_rows.at[:, :, pl.ds(pl.multiple_of(tile * LANES, LANES), LANES)],
            dst_ref=left_cols.at[:, chip_rows, :],
            send_sem=left_send.at[index],
            recv_sem=left_recv.at[chip],
            device_id=(to_grp, to_inner),
            device_id_type=MESH,
        )
        return to_grp * 2 + to_inner // 2 != chip, copy

    def send_left():
        swap.wait_recv()

        @pl.when(core == 0)
        def _():
            merge(own, sib)

        @pl.when(core == 1)
        def _():
            merge(sib, own)

        @pl.loop(0, tiles // 2)
        def _(step):
            index = (step + 3 * (grp // 2)) % (tiles // 2)
            away, copy = left_copy(index)

            @pl.when(away)
            def _():
                copy.start()

    def relay(step):
        z_of = flip_z(z, step)
        arrived(X1 + step, z_of, y, 1 - x, 0, half)
        send(Y2 + step, z_of, y, 1 - x, 0, quarter, y_side)
        send(CX + step, z_of, y, 1 - x, 0, half, sibling)
        arrived(Y1 + step, z_of, 1 - y, x, 0, half)
        send(X2 + step, z_of, 1 - y, x, quarter, quarter, x_side)
        send(CY + step, z_of, 1 - y, x, 0, half, sibling)

    def finish(step):
        z_of = flip_z(z, step)
        arrived(Y2 + step, z_of, 1 - y, 1 - x, 0, quarter)
        arrived(X2 + step, z_of, 1 - y, 1 - x, quarter, quarter)
        send(CD + step, z_of, 1 - y, 1 - x, 0, half, sibling)

    for step in (1, 2, 3):
        z_of = flip_z(z, step)
        arrived(Z + step, z_of, y, x, 0, half)
        spread(step)
        send(CZ + step, z_of, y, x, 0, half, sibling)
        relay(step - 1)
        if step == 2:
            send_left()
        if step > 1:
            finish(step - 2)
    relay(3)
    finish(2)
    finish(3)
    for step in range(4):
        z_of = flip_z(z, step)
        arrived(CZ + step, z_of, y, x, 0, half, 1 - core)
        arrived(CX + step, z_of, y, 1 - x, 0, half, 1 - core)
        arrived(CY + step, z_of, 1 - y, x, 0, half, 1 - core)
        arrived(CD + step, z_of, 1 - y, 1 - x, 0, half, 1 - core)

    idle = 2 * ((z + y) % 2) + 1
    my_tile = grp * 3 + inner - jnp.where(inner > idle, 1, 0)
    my_lanes = pl.ds(pl.multiple_of(my_tile * LANES, LANES), LANES)

    def out_copy(step):
        other = (me + step) % 32
        return pltpu.make_async_remote_copy(
            src_ref=contrib.at[:, pl.ds(pl.multiple_of(other * 8, 8), 8), :],
            dst_ref=out_ref.at[:, :, my_lanes],
            send_sem=out_send.at[step],
            recv_sem=out_recv.at[my_tile],
            device_id=(other // 4, other % 4),
            device_id_type=MESH,
        )

    @pl.when(inner != idle)
    def _():
        left_cols[:, chip_rows, :] = pair_rows[:, :, my_lanes]

        @pl.loop(1, 16)
        def _(step):
            source = (chip + step) % 16
            pltpu.make_async_remote_copy(
                src_ref=pair_rows.at[:, :, pl.ds(0, LANES)],
                dst_ref=left_cols.at[:, pl.ds(pl.multiple_of(source * 16, 16), 16), :],
                send_sem=left_send.at[0],
                recv_sem=left_recv.at[source],
                device_id=sibling,
                device_id_type=MESH,
            ).wait_recv()

        vir_cols = jnp.transpose(jnp.broadcast_to(vir_ref[:, my_lanes], (LANES, LANES)))[:, :1]
        shifts = []
        for pair in range(pairs):
            left_rows[pl.ds(pair * LANES, LANES), :] = jnp.transpose(left_cols[pair])
            shifts.append((occ_ref[left_ref[pair]] + occ_ref[second]) - vir_cols)
        shift = jnp.concatenate(shifts, axis=0)
        wide = 4 * LANES
        total = jnp.zeros((pairs * LANES, left_rows.shape[1]), jnp.float32)
        for part in range(virtuals // wide):
            columns = pl.ds(part * wide, wide)
            side, first = divmod(part * wide, half)
            both = full[:, :, pl.ds(first, wide)].astype(jnp.float32)
            block = both[:, 8 * side : 8 * side + 8].reshape(left_rows.shape[1], wide).astype(jnp.bfloat16)
            integral = jnp.dot(left_rows[...], block, preferred_element_type=jnp.float32)
            denominator = shift - vir_ref[:, columns]
            inverse = pl.reciprocal(denominator, approx=True)
            inverse = inverse * (2.0 - denominator * inverse)
            amplitude = (integral * inverse).astype(jnp.bfloat16)
            total += lax.dot_general(
                amplitude, block, (((1,), (1,)), ((), ())), preferred_element_type=jnp.float32
            )
        for pair in range(pairs):
            contrib[pair] = jnp.transpose(total[pair * LANES : (pair + 1) * LANES])

        out_ref[:, :, my_lanes] = contrib[:, pl.ds(pl.multiple_of(me * 8, 8), 8), :]

        @pl.loop(1, 32)
        def _(step):
            out_copy(step).start()

    swap.wait_send()
    for copy in started:
        copy.wait_send()

    @pl.loop(0, tiles // 2)
    def _(index):
        away, copy = left_copy(index)

        @pl.when(away)
        def _():
            copy.wait_send()

    @pl.loop(0, tiles)
    def _(tile):
        from_grp, from_inner = tile_owner(tile)

        @pl.when(from_grp * 4 + from_inner != me)
        def _():
            pltpu.make_async_remote_copy(
                src_ref=contrib.at[:, pl.ds(0, 8), :],
                dst_ref=out_ref.at[:, :, pl.ds(pl.multiple_of(tile * LANES, LANES), LANES)],
                send_sem=out_send.at[0],
                recv_sem=out_recv.at[tile],
                device_id=sibling,
                device_id_type=MESH,
            ).wait_recv()

    @pl.when(inner != idle)
    def _():
        @pl.loop(1, 32)
        def _(step):
            out_copy(step).wait_send()


def body_tiles(b_tensor, occ_energy, vir_energy, left_list, right_occ):
    occ_count, aux_rows, virtuals = b_tensor.shape
    pairs = left_list.shape[0]
    aux = 32 * aux_rows
    hbm, vmem = pl.BlockSpec(memory_space=pltpu.HBM), pl.BlockSpec(memory_space=pltpu.VMEM)
    dma = pltpu.SemaphoreType.DMA
    returned = pl.pallas_call(
        kernel,
        out_shape=jax.ShapeDtypeStruct((pairs, aux_rows, virtuals), jnp.float32),
        in_specs=[hbm] * 5,
        out_specs=vmem,
        scratch_shapes=[
            pltpu.VMEM(b_tensor.shape, jnp.bfloat16),
            pltpu.SMEM(occ_energy.shape, jnp.float32),
            pltpu.VMEM((1, virtuals), jnp.float32),
            pltpu.SMEM(left_list.shape, jnp.int32),
            pltpu.SMEM(right_occ.shape, jnp.int32),
            dma((5,)),
            pltpu.VMEM(((pairs + 1) * aux_rows, virtuals), jnp.bfloat16),
            pltpu.VMEM(((pairs + 1) * aux_rows, virtuals), jnp.bfloat16),
            pltpu.VMEM((2 * aux_rows, virtuals // 2), jnp.bfloat16),
            pltpu.VMEM((pairs, 2 * aux_rows, virtuals), jnp.bfloat16),
            pltpu.VMEM((32, 2 * aux_rows, virtuals // 2), jnp.bfloat16),
            pltpu.VMEM((pairs, aux, LANES), jnp.bfloat16),
            pltpu.VMEM((pairs * LANES, aux), jnp.bfloat16),
            pltpu.VMEM((pairs, aux, LANES), jnp.float32),
            dma, dma, dma((36,)), dma((36,)), dma((virtuals // LANES,)), dma((16,)),
            dma((32,)), dma((virtuals // LANES,)),
        ],
        compiler_params=pltpu.CompilerParams(
            collective_id=0, has_side_effects=True, vmem_limit_bytes=60 * 2**20
        ),
        cost_estimate=pl.CostEstimate(
            flops=4 * pairs * aux * virtuals * LANES, bytes_accessed=2 * occ_count * aux_rows * virtuals, transcendentals=0
        ),
    )(b_tensor, occ_energy, vir_energy.reshape(1, virtuals), left_list, right_occ)
    orbitals = lax.broadcasted_iota(jnp.int32, (occ_count,) + returned.shape, 0)
    chosen = orbitals == left_list[None, :, None, None]
    return jnp.sum(jnp.where(chosen, returned[None], 0.0), axis=1)


def solution(mesh):
    placed = (P(None, ("grp", "inner"), None), P(), P(), P(), P())
    plan = body
    if mesh.shape["grp"] == 8 and mesh.shape["inner"] == 4:
        plan = body_tiles

    def program(b_tensor, *rest):
        aux, virtuals = b_tensor.shape[1:]
        fits = aux == 256 and virtuals == 3072
        return jax.shard_map(
            plan if fits else body,
            mesh=mesh,
            in_specs=placed,
            out_specs=P(None, ("grp", "inner"), None),
            check_vma=False,
        )(b_tensor, *rest)

    return program
```

```python
import jax
import jax.numpy as jnp
from jax import lax
from jax.experimental import pallas as pl
from jax.experimental.pallas import tpu as pltpu
from jax.sharding import PartitionSpec as P

MESH = pl.DeviceIdType.MESH
LANES = 128


def body(b_tensor, occ_energy, vir_energy, left_list, right_occ):
    inner_size = lax.axis_size("inner")
    group_size = lax.axis_size("grp")
    occ_count = b_tensor.shape[0]
    virtuals = b_tensor.shape[2]
    row_count = virtuals // inner_size
    col_count = virtuals // group_size
    inner_rank = lax.axis_index("inner")
    group_rank = lax.axis_index("grp")
    vir_rows = lax.dynamic_slice_in_dim(vir_energy, inner_rank * row_count, row_count)
    vir_cols = lax.dynamic_slice_in_dim(vir_energy, group_rank * col_count, col_count)
    gamma_aux = jnp.zeros(b_tensor.shape, jnp.float32)
    orbitals = jnp.arange(occ_count, dtype=jnp.int32)
    second_occ = right_occ[0]
    block_right = lax.dynamic_index_in_dim(b_tensor, second_occ, 0, keepdims=False)
    right_full = lax.all_gather(block_right, "inner", axis=0, tiled=True)
    pair_total = left_list.shape[0]
    selectors = []
    shifts = []
    partials = []
    amp_list = []
    for pair_no in range(pair_total):
        left_occ = left_list[pair_no]
        block_left = lax.dynamic_index_in_dim(b_tensor, left_occ, 0, keepdims=False)
        left_rows = lax.all_to_all(block_left, "inner", split_axis=1, concat_axis=0, tiled=True)
        partial_value = lax.dot_general(
            left_rows, right_full, (((0,), (0,)), ((), ())), preferred_element_type=jnp.float32
        )
        shift_occ = occ_energy[left_occ] + occ_energy[second_occ]
        selectors.append((orbitals == left_occ).astype(jnp.float32))
        partials.append(partial_value)
        shifts.append(shift_occ)
    stacked = jnp.stack(partials, axis=0)
    shares_all = lax.psum_scatter(stacked, "grp", scatter_dimension=2, tiled=True)
    shift_all = jnp.stack(shifts, axis=0)
    denominator_all = shift_all[:, None, None] - vir_rows[None, :, None] - vir_cols[None, None, :]
    amp_tiles = (shares_all / denominator_all).astype(jnp.bfloat16)
    amp_whole = lax.all_gather(amp_tiles, "grp", axis=2, tiled=True)
    amp_list = [amp_whole[pair_no] for pair_no in range(pair_total)]
    for pair_no in range(pair_total):
        contrib = lax.dot_general(
            right_full,
            amp_list[pair_no],
            (((1,), (1,)), ((), ())),
            preferred_element_type=jnp.float32,
        )
        returned = lax.all_to_all(contrib, "inner", split_axis=0, concat_axis=1, tiled=True)
        gamma_aux = gamma_aux + selectors[pair_no][:, None, None] * returned[None]
    return gamma_aux


def place(grp, inner):
    return grp // 2, grp % 2, inner // 2, inner % 2


def tile_owner(tile):
    grp = tile // 3
    slot = tile % 3
    idle = 2 * ((grp // 2 + grp % 2) % 2) + 1
    return grp, slot + jnp.where(slot >= idle, 1, 0)


def flip_z(z, step):
    return (z, z + 1 - 2 * (z % 2), (z + 2) % 4, 3 - z)[step]


def kernel(
    b_hbm, occ_hbm, vir_hbm, left_hbm, right_hbm, out_ref,
    b_ref, occ_ref, vir_ref, left_ref, right_ref, input_sem, own, sib, folded, pair_rows, full, left_cols, left_rows, contrib,
    swap_send, swap_recv, gather_send, gather_recv, left_send, left_recv, out_send, out_recv,
):
    grp, inner = lax.axis_index("grp"), lax.axis_index("inner")
    z, y, x, core = place(grp, inner)
    me = grp * 4 + inner
    chip = grp * 2 + x
    pairs = out_ref.shape[0]
    half = full.shape[2]
    virtuals = 2 * half
    quarter = half // 2
    tiles = virtuals // LANES

    inputs = ((b_hbm, b_ref), (occ_hbm, occ_ref), (vir_hbm, vir_ref), (left_hbm, left_ref), (right_hbm, right_ref))
    fetches = [pltpu.make_async_copy(a, b, input_sem.at[n]) for n, (a, b) in enumerate(inputs)]
    for fetch in fetches:
        fetch.start()
    barrier = pltpu.get_barrier_semaphore()

    @pl.loop(1, 32)
    def _(step):
        other = (me + step) % 32
        pl.semaphore_signal(barrier, inc=1, device_id=(other // 4, other % 4), device_id_type=MESH)

    for fetch in fetches:
        fetch.wait()
    second = right_ref[0]
    folded[pl.ds(0, 8), :] = b_ref[second, :, pl.ds(0, half)]
    folded[pl.ds(8, 8), :] = b_ref[second, :, pl.ds(half, half)]
    full[me] = folded[...]
    own[pl.ds(0, 8), :] = b_ref[second]
    for pair in range(pairs):
        own[pl.ds(8 * pair + 8, 8), :] = b_ref[left_ref[pair]]
    pl.semaphore_wait(barrier, 31)

    sibling = (grp, inner + 1 - 2 * core)
    swap = pltpu.make_async_remote_copy(
        src_ref=own, dst_ref=sib, send_sem=swap_send, recv_sem=swap_recv, device_id=sibling, device_id_type=MESH
    )

    x_side = (grp, (1 - x) * 2 + core)
    y_side = (z * 2 + 1 - y, inner)
    started = []

    def send(slot, z_of, y_of, x_of, first, count, target):
        piece = full.at[(z_of * 2 + y_of) * 4 + x_of * 2 + core, :, pl.ds(first, count)]
        copy = pltpu.make_async_remote_copy(
            src_ref=piece, dst_ref=piece, send_sem=gather_send.at[slot], recv_sem=gather_recv.at[slot],
            device_id=target, device_id_type=MESH,
        )
        copy.start()
        started.append(copy)

    def arrived(slot, z_of, y_of, x_of, first, count, side=core):
        piece = full.at[(z_of * 2 + y_of) * 4 + x_of * 2 + side, :, pl.ds(first, count)]
        pltpu.make_async_remote_copy(
            src_ref=piece, dst_ref=piece, send_sem=gather_send.at[slot], recv_sem=gather_recv.at[slot],
            device_id=sibling, device_id_type=MESH,
        ).wait_recv()

    Z, X1, Y1, X2, Y2, CZ, CX, CY, CD = 0, 4, 8, 12, 16, 20, 24, 28, 32

    def spread(step):
        z_of = flip_z(z, step)
        send(X1 + step, z_of, y, x, 0, half, x_side)
        send(Y1 + step, z_of, y, x, 0, half, y_side)

    for step in (1, 2, 3):
        send(Z + step, z, y, x, 0, half, (flip_z(z, step) * 2 + y, inner))
    spread(0)
    send(CZ, z, y, x, 0, half, sibling)
    swap.start()

    def merge(low, high):
        for block in range(pairs):
            pair_rows[block, pl.ds(0, 8), :] = low[pl.ds(8 * block + 8, 8), :]
            pair_rows[block, pl.ds(8, 8), :] = high[pl.ds(8 * block + 8, 8), :]

    chip_rows = pl.ds(pl.multiple_of(chip * 16, 16), 16)

    def left_copy(index):
        tile = 2 * index + core
        to_grp, to_inner = tile_owner(tile)
        copy = pltpu.make_async_remote_copy(
            src_ref=pair_rows.at[:, :, pl.ds(pl.multiple_of(tile * LANES, LANES), LANES)],
            dst_ref=left_cols.at[:, chip_rows, :],
            send_sem=left_send.at[index],
            recv_sem=left_recv.at[chip],
            device_id=(to_grp, to_inner),
            device_id_type=MESH,
        )
        return to_grp * 2 + to_inner // 2 != chip, copy

    def send_left():
        swap.wait_recv()

        @pl.when(core == 0)
        def _():
            merge(own, sib)

        @pl.when(core == 1)
        def _():
            merge(sib, own)

        @pl.loop(0, tiles // 2)
        def _(step):
            index = (5 * step + 3 * z) % (tiles // 2)
            away, copy = left_copy(index)

            @pl.when(away)
            def _():
                copy.start()

    def relay(step):
        z_of = flip_z(z, step)
        arrived(X1 + step, z_of, y, 1 - x, 0, half)
        send(Y2 + step, z_of, y, 1 - x, 0, quarter, y_side)
        send(CX + step, z_of, y, 1 - x, 0, half, sibling)
        arrived(Y1 + step, z_of, 1 - y, x, 0, half)
        send(X2 + step, z_of, 1 - y, x, quarter, quarter, x_side)
        send(CY + step, z_of, 1 - y, x, 0, half, sibling)

    def finish(step):
        z_of = flip_z(z, step)
        arrived(Y2 + step, z_of, 1 - y, 1 - x, 0, quarter)
        arrived(X2 + step, z_of, 1 - y, 1 - x, quarter, quarter)
        send(CD + step, z_of, 1 - y, 1 - x, 0, half, sibling)

    for step in (1, 2, 3):
        z_of = flip_z(z, step)
        arrived(Z + step, z_of, y, x, 0, half)
        spread(step)
        send(CZ + step, z_of, y, x, 0, half, sibling)
        relay(step - 1)
        if step == 2:
            send_left()
        if step > 1:
            finish(step - 2)
    relay(3)
    finish(2)
    finish(3)
    for step in range(4):
        z_of = flip_z(z, step)
        arrived(CZ + step, z_of, y, x, 0, half, 1 - core)
        arrived(CX + step, z_of, y, 1 - x, 0, half, 1 - core)
        arrived(CY + step, z_of, 1 - y, x, 0, half, 1 - core)
        arrived(CD + step, z_of, 1 - y, 1 - x, 0, half, 1 - core)

    idle = 2 * ((z + y) % 2) + 1
    my_tile = grp * 3 + inner - jnp.where(inner > idle, 1, 0)
    my_lanes = pl.ds(pl.multiple_of(my_tile * LANES, LANES), LANES)

    def out_copy(step):
        other = (me + 11 * step) % 32
        return pltpu.make_async_remote_copy(
            src_ref=contrib.at[:, pl.ds(pl.multiple_of(other * 8, 8), 8), :],
            dst_ref=out_ref.at[:, :, my_lanes],
            send_sem=out_send.at[step],
            recv_sem=out_recv.at[my_tile],
            device_id=(other // 4, other % 4),
            device_id_type=MESH,
        )

    @pl.when(inner != idle)
    def _():
        left_cols[:, chip_rows, :] = pair_rows[:, :, my_lanes]

        @pl.loop(1, 16)
        def _(step):
            source = (chip + step) % 16
            pltpu.make_async_remote_copy(
                src_ref=pair_rows.at[:, :, pl.ds(0, LANES)],
                dst_ref=left_cols.at[:, pl.ds(pl.multiple_of(source * 16, 16), 16), :],
                send_sem=left_send.at[0],
                recv_sem=left_recv.at[source],
                device_id=sibling,
                device_id_type=MESH,
            ).wait_recv()

        vir_cols = jnp.transpose(jnp.broadcast_to(vir_ref[:, my_lanes], (LANES, LANES)))[:, :1]
        shifts = []
        for pair in range(pairs):
            left_rows[pl.ds(pair * LANES, LANES), :] = jnp.transpose(left_cols[pair])
            shifts.append((occ_ref[left_ref[pair]] + occ_ref[second]) - vir_cols)
        shift = jnp.concatenate(shifts, axis=0)
        wide = 4 * LANES
        total = jnp.zeros((pairs * LANES, left_rows.shape[1]), jnp.float32)
        for part in range(virtuals // wide):
            columns = pl.ds(part * wide, wide)
            side, first = divmod(part * wide, half)
            both = full[:, :, pl.ds(first, wide)].astype(jnp.float32)
            block = both[:, 8 * side : 8 * side + 8].reshape(left_rows.shape[1], wide).astype(jnp.bfloat16)
            integral = jnp.dot(left_rows[...], block, preferred_element_type=jnp.float32)
            denominator = shift - vir_ref[:, columns]
            inverse = pl.reciprocal(denominator, approx=True)
            inverse = inverse * (2.0 - denominator * inverse)
            amplitude = (integral * inverse).astype(jnp.bfloat16)
            total += lax.dot_general(
                amplitude, block, (((1,), (1,)), ((), ())), preferred_element_type=jnp.float32
            )
        for pair in range(pairs):
            contrib[pair] = jnp.transpose(total[pair * LANES : (pair + 1) * LANES])

        out_ref[:, :, my_lanes] = contrib[:, pl.ds(pl.multiple_of(me * 8, 8), 8), :]

        @pl.loop(1, 32)
        def _(step):
            out_copy(step).start()

    swap.wait_send()
    for copy in started:
        copy.wait_send()

    @pl.loop(0, tiles // 2)
    def _(index):
        away, copy = left_copy(index)

        @pl.when(away)
        def _():
            copy.wait_send()

    @pl.loop(0, tiles)
    def _(tile):
        from_grp, from_inner = tile_owner(tile)

        @pl.when(from_grp * 4 + from_inner != me)
        def _():
            pltpu.make_async_remote_copy(
                src_ref=contrib.at[:, pl.ds(0, 8), :],
                dst_ref=out_ref.at[:, :, pl.ds(pl.multiple_of(tile * LANES, LANES), LANES)],
                send_sem=out_send.at[0],
                recv_sem=out_recv.at[tile],
                device_id=sibling,
                device_id_type=MESH,
            ).wait_recv()

    @pl.when(inner != idle)
    def _():
        @pl.loop(1, 32)
        def _(step):
            out_copy(step).wait_send()


def add_pairs(left_ref, returned_ref, gamma_ref, rows, sems):
    copies = []
    for orbital in range(rows.shape[0]):
        row = jnp.where(left_ref[0] == orbital, returned_ref[0], 0.0)
        for pair in range(1, returned_ref.shape[0]):
            row += jnp.where(left_ref[pair] == orbital, returned_ref[pair], 0.0)
        rows[orbital] = row
        copies.append(pltpu.make_async_copy(rows.at[orbital], gamma_ref.at[orbital], sems.at[orbital]))
        copies[-1].start()
    for copy in copies:
        copy.wait()


def body_tiles(b_tensor, occ_energy, vir_energy, left_list, right_occ):
    occ_count, aux_rows, virtuals = b_tensor.shape
    pairs = left_list.shape[0]
    aux = 32 * aux_rows
    hbm, vmem = pl.BlockSpec(memory_space=pltpu.HBM), pl.BlockSpec(memory_space=pltpu.VMEM)
    dma = pltpu.SemaphoreType.DMA
    returned = pl.pallas_call(
        kernel,
        out_shape=jax.ShapeDtypeStruct((pairs, aux_rows, virtuals), jnp.float32),
        in_specs=[hbm] * 5,
        out_specs=vmem,
        scratch_shapes=[
            pltpu.VMEM(b_tensor.shape, jnp.bfloat16),
            pltpu.SMEM(occ_energy.shape, jnp.float32),
            pltpu.VMEM((1, virtuals), jnp.float32),
            pltpu.SMEM(left_list.shape, jnp.int32),
            pltpu.SMEM(right_occ.shape, jnp.int32),
            dma((5,)),
            pltpu.VMEM(((pairs + 1) * aux_rows, virtuals), jnp.bfloat16),
            pltpu.VMEM(((pairs + 1) * aux_rows, virtuals), jnp.bfloat16),
            pltpu.VMEM((2 * aux_rows, virtuals // 2), jnp.bfloat16),
            pltpu.VMEM((pairs, 2 * aux_rows, virtuals), jnp.bfloat16),
            pltpu.VMEM((32, 2 * aux_rows, virtuals // 2), jnp.bfloat16),
            pltpu.VMEM((pairs, aux, LANES), jnp.bfloat16),
            pltpu.VMEM((pairs * LANES, aux), jnp.bfloat16),
            pltpu.VMEM((pairs, aux, LANES), jnp.float32),
            dma, dma, dma((36,)), dma((36,)), dma((virtuals // LANES,)), dma((16,)),
            dma((32,)), dma((virtuals // LANES,)),
        ],
        compiler_params=pltpu.CompilerParams(
            collective_id=0, has_side_effects=True, vmem_limit_bytes=60 * 2**20
        ),
        cost_estimate=pl.CostEstimate(
            flops=4 * pairs * aux * virtuals * LANES, bytes_accessed=2 * occ_count * aux_rows * virtuals, transcendentals=0
        ),
    )(b_tensor, occ_energy, vir_energy.reshape(1, virtuals), left_list, right_occ)
    return pl.pallas_call(
        add_pairs,
        out_shape=jax.ShapeDtypeStruct(b_tensor.shape, jnp.float32),
        in_specs=[pl.BlockSpec(memory_space=pltpu.SMEM), vmem],
        out_specs=hbm,
        scratch_shapes=[pltpu.VMEM(b_tensor.shape, jnp.float32), dma((occ_count,))],
    )(left_list, returned)


def solution(mesh):
    placed = (P(None, ("grp", "inner"), None), P(), P(), P(), P())
    plan = body
    if mesh.shape["grp"] == 8 and mesh.shape["inner"] == 4:
        plan = body_tiles

    def program(b_tensor, *rest):
        aux, virtuals = b_tensor.shape[1:]
        fits = aux == 256 and virtuals == 3072
        return jax.shard_map(
            plan if fits else body,
            mesh=mesh,
            in_specs=placed,
            out_specs=P(None, ("grp", "inner"), None),
            check_vma=False,
        )(b_tensor, *rest)

    return program
```

```python
import jax
import jax.numpy as jnp
from jax import lax
from jax.experimental import pallas as pl
from jax.experimental.pallas import tpu as pltpu
from jax.sharding import PartitionSpec as P

MESH = pl.DeviceIdType.MESH
LANES = 128


def body(b_tensor, occ_energy, vir_energy, left_list, right_occ):
    inner_size = lax.axis_size("inner")
    group_size = lax.axis_size("grp")
    occ_count = b_tensor.shape[0]
    virtuals = b_tensor.shape[2]
    row_count = virtuals // inner_size
    col_count = virtuals // group_size
    inner_rank = lax.axis_index("inner")
    group_rank = lax.axis_index("grp")
    vir_rows = lax.dynamic_slice_in_dim(vir_energy, inner_rank * row_count, row_count)
    vir_cols = lax.dynamic_slice_in_dim(vir_energy, group_rank * col_count, col_count)
    gamma_aux = jnp.zeros(b_tensor.shape, jnp.float32)
    orbitals = jnp.arange(occ_count, dtype=jnp.int32)
    second_occ = right_occ[0]
    block_right = lax.dynamic_index_in_dim(b_tensor, second_occ, 0, keepdims=False)
    right_full = lax.all_gather(block_right, "inner", axis=0, tiled=True)
    pair_total = left_list.shape[0]
    selectors = []
    shifts = []
    partials = []
    amp_list = []
    for pair_no in range(pair_total):
        left_occ = left_list[pair_no]
        block_left = lax.dynamic_index_in_dim(b_tensor, left_occ, 0, keepdims=False)
        left_rows = lax.all_to_all(block_left, "inner", split_axis=1, concat_axis=0, tiled=True)
        partial_value = lax.dot_general(
            left_rows, right_full, (((0,), (0,)), ((), ())), preferred_element_type=jnp.float32
        )
        shift_occ = occ_energy[left_occ] + occ_energy[second_occ]
        selectors.append((orbitals == left_occ).astype(jnp.float32))
        partials.append(partial_value)
        shifts.append(shift_occ)
    stacked = jnp.stack(partials, axis=0)
    shares_all = lax.psum_scatter(stacked, "grp", scatter_dimension=2, tiled=True)
    shift_all = jnp.stack(shifts, axis=0)
    denominator_all = shift_all[:, None, None] - vir_rows[None, :, None] - vir_cols[None, None, :]
    amp_tiles = (shares_all / denominator_all).astype(jnp.bfloat16)
    amp_whole = lax.all_gather(amp_tiles, "grp", axis=2, tiled=True)
    amp_list = [amp_whole[pair_no] for pair_no in range(pair_total)]
    for pair_no in range(pair_total):
        contrib = lax.dot_general(
            right_full,
            amp_list[pair_no],
            (((1,), (1,)), ((), ())),
            preferred_element_type=jnp.float32,
        )
        returned = lax.all_to_all(contrib, "inner", split_axis=0, concat_axis=1, tiled=True)
        gamma_aux = gamma_aux + selectors[pair_no][:, None, None] * returned[None]
    return gamma_aux


def place(grp, inner):
    z, x = lax.div(grp, 2), lax.div(inner, 2)
    return z, grp - 2 * z, x, inner - 2 * x


def idle_inner(z, y):
    return 2 * lax.rem(z + y, 2) + 1


def flip_z(z, step):
    return (z, z + 1 - 2 * lax.rem(z, 2), lax.rem(z + 2, 4), 3 - z)[step]


def kernel(
    b_hbm, occ_hbm, vir_hbm, left_hbm, right_hbm, out_ref,
    b_ref, occ_ref, vir_ref, left_ref, right_ref, input_sem, own, sib, folded, pair_rows, full, left_cols, left_rows, contrib,
    swap_send, swap_recv, gather_send, gather_recv, left_send, left_recv, out_send, out_recv,
):
    grp, inner = lax.axis_index("grp"), lax.axis_index("inner")
    z, y, x, core = place(grp, inner)
    me = grp * 4 + inner
    chip = grp * 2 + x
    pairs = out_ref.shape[0]
    half = full.shape[2]
    virtuals = 2 * half
    quarter = half // 2
    tiles = virtuals // LANES

    inputs = ((b_hbm, b_ref), (occ_hbm, occ_ref), (vir_hbm, vir_ref), (left_hbm, left_ref), (right_hbm, right_ref))
    fetches = [pltpu.make_async_copy(a, b, input_sem.at[n]) for n, (a, b) in enumerate(inputs)]
    for fetch in fetches:
        fetch.start()
    barrier = pltpu.get_barrier_semaphore()

    @pl.loop(0, 8)
    def _(to_grp):
        for to_inner in range(4):

            @pl.when(to_grp * 4 + to_inner != me)
            def _():
                pl.semaphore_signal(barrier, inc=1, device_id=(to_grp, to_inner), device_id_type=MESH)

    for fetch in fetches:
        fetch.wait()
    second = right_ref[0]
    folded[pl.ds(0, 8), :] = b_ref[second, :, pl.ds(0, half)]
    folded[pl.ds(8, 8), :] = b_ref[second, :, pl.ds(half, half)]
    full[me] = folded[...]
    own[pl.ds(0, 8), :] = b_ref[second]
    for pair in range(pairs):
        own[pl.ds(8 * pair + 8, 8), :] = b_ref[left_ref[pair]]
    pl.semaphore_wait(barrier, 31)

    sibling = (grp, inner + 1 - 2 * core)
    swap = pltpu.make_async_remote_copy(
        src_ref=own, dst_ref=sib, send_sem=swap_send, recv_sem=swap_recv, device_id=sibling, device_id_type=MESH
    )

    x_side = (grp, (1 - x) * 2 + core)
    y_side = (z * 2 + 1 - y, inner)
    started = []

    def send(slot, z_of, y_of, x_of, first, count, target):
        piece = full.at[(z_of * 2 + y_of) * 4 + x_of * 2 + core, :, pl.ds(first, count)]
        copy = pltpu.make_async_remote_copy(
            src_ref=piece, dst_ref=piece, send_sem=gather_send.at[slot], recv_sem=gather_recv.at[slot],
            device_id=target, device_id_type=MESH,
        )
        copy.start()
        started.append(copy)

    def arrived(slot, z_of, y_of, x_of, first, count, side=core):
        piece = full.at[(z_of * 2 + y_of) * 4 + x_of * 2 + side, :, pl.ds(first, count)]
        pltpu.make_async_remote_copy(
            src_ref=piece, dst_ref=piece, send_sem=gather_send.at[slot], recv_sem=gather_recv.at[slot],
            device_id=sibling, device_id_type=MESH,
        ).wait_recv()

    Z, X1, Y1, X2, Y2, CZ, CX, CY, CD = 0, 4, 8, 12, 16, 20, 24, 28, 32

    def spread(step):
        z_of = flip_z(z, step)
        send(X1 + step, z_of, y, x, 0, half, x_side)
        send(Y1 + step, z_of, y, x, 0, half, y_side)

    for step in (1, 2, 3):
        send(Z + step, z, y, x, 0, half, (flip_z(z, step) * 2 + y, inner))
    spread(0)
    send(CZ, z, y, x, 0, half, sibling)
    swap.start()

    def merge(low, high):
        for block in range(pairs):
            pair_rows[block, pl.ds(0, 8), :] = low[pl.ds(8 * block + 8, 8), :]
            pair_rows[block, pl.ds(8, 8), :] = high[pl.ds(8 * block + 8, 8), :]

    chip_rows = pl.ds(pl.multiple_of(chip * 16, 16), 16)

    def for_left(act):
        for side in range(2):

            @pl.when(core == side)
            def _():
                @pl.loop(0, 4)
                def _(step):
                    to_z = lax.rem(z + step, 4)
                    for to_y in range(2):
                        for slot in range(3):
                            if (to_y + slot) % 2 != side:
                                continue
                            to_grp = 2 * to_z + to_y
                            tile = 3 * to_grp + slot
                            to_inner = slot + jnp.where(slot >= idle_inner(to_z, to_y), 1, 0)
                            copy = pltpu.make_async_remote_copy(
                                src_ref=pair_rows.at[:, :, pl.ds(pl.multiple_of(tile * LANES, LANES), LANES)],
                                dst_ref=left_cols.at[:, chip_rows, :],
                                send_sem=left_send.at[tile],
                                recv_sem=left_recv.at[chip],
                                device_id=(to_grp, to_inner),
                                device_id_type=MESH,
                            )

                            @pl.when(to_grp * 2 + lax.div(to_inner, 2) != chip)
                            def _():
                                act(copy)

    def send_left():
        swap.wait_recv()

        @pl.when(core == 0)
        def _():
            merge(own, sib)

        @pl.when(core == 1)
        def _():
            merge(sib, own)

        for_left(lambda copy: copy.start())

    def relay(step):
        z_of = flip_z(z, step)
        arrived(X1 + step, z_of, y, 1 - x, 0, half)
        send(Y2 + step, z_of, y, 1 - x, 0, quarter, y_side)
        send(CX + step, z_of, y, 1 - x, 0, half, sibling)
        arrived(Y1 + step, z_of, 1 - y, x, 0, half)
        send(X2 + step, z_of, 1 - y, x, quarter, quarter, x_side)
        send(CY + step, z_of, 1 - y, x, 0, half, sibling)

    def finish(step):
        z_of = flip_z(z, step)
        arrived(Y2 + step, z_of, 1 - y, 1 - x, 0, quarter)
        arrived(X2 + step, z_of, 1 - y, 1 - x, quarter, quarter)
        send(CD + step, z_of, 1 - y, 1 - x, 0, half, sibling)

    for step in (1, 2, 3):
        z_of = flip_z(z, step)
        arrived(Z + step, z_of, y, x, 0, half)
        spread(step)
        send(CZ + step, z_of, y, x, 0, half, sibling)
        if step == 3:
            send_left()
        relay(step - 1)
        if step > 1:
            finish(step - 2)
    relay(3)
    finish(2)
    finish(3)
    for step in range(4):
        z_of = flip_z(z, step)
        arrived(CZ + step, z_of, y, x, 0, half, 1 - core)
        arrived(CX + step, z_of, y, 1 - x, 0, half, 1 - core)
        arrived(CY + step, z_of, 1 - y, x, 0, half, 1 - core)
        arrived(CD + step, z_of, 1 - y, 1 - x, 0, half, 1 - core)

    idle = idle_inner(z, y)
    my_tile = grp * 3 + inner - jnp.where(inner > idle, 1, 0)
    my_lanes = pl.ds(pl.multiple_of(my_tile * LANES, LANES), LANES)

    def for_out(act):
        @pl.loop(0, 8)
        def _(step):
            to_grp = lax.rem(grp + step, 8)
            for to_inner in range(4):
                other = to_grp * 4 + to_inner
                copy = pltpu.make_async_remote_copy(
                    src_ref=contrib.at[:, pl.ds(pl.multiple_of(other * 8, 8), 8), :],
                    dst_ref=out_ref.at[:, :, my_lanes],
                    send_sem=out_send.at[other],
                    recv_sem=out_recv.at[my_tile],
                    device_id=(to_grp, to_inner),
                    device_id_type=MESH,
                )

                @pl.when(other != me)
                def _():
                    act(copy)

    @pl.when(inner != idle)
    def _():
        left_cols[:, chip_rows, :] = pair_rows[:, :, my_lanes]

        @pl.loop(1, 16)
        def _(step):
            source = lax.rem(chip + step, 16)
            pltpu.make_async_remote_copy(
                src_ref=pair_rows.at[:, :, pl.ds(0, LANES)],
                dst_ref=left_cols.at[:, pl.ds(pl.multiple_of(source * 16, 16), 16), :],
                send_sem=left_send.at[0],
                recv_sem=left_recv.at[source],
                device_id=sibling,
                device_id_type=MESH,
            ).wait_recv()

        vir_cols = jnp.transpose(jnp.broadcast_to(vir_ref[:, my_lanes], (LANES, LANES)))[:, :1]
        shifts = []
        for pair in range(pairs):
            left_rows[pl.ds(pair * LANES, LANES), :] = jnp.transpose(left_cols[pair])
            shifts.append((occ_ref[left_ref[pair]] + occ_ref[second]) - vir_cols)
        shift = jnp.concatenate(shifts, axis=0)
        wide = 4 * LANES
        total = jnp.zeros((pairs * LANES, left_rows.shape[1]), jnp.float32)
        for part in range(virtuals // wide):
            columns = pl.ds(part * wide, wide)
            side, first = divmod(part * wide, half)
            both = full[:, :, pl.ds(first, wide)].astype(jnp.float32)
            block = both[:, 8 * side : 8 * side + 8].reshape(left_rows.shape[1], wide).astype(jnp.bfloat16)
            integral = jnp.dot(left_rows[...], block, preferred_element_type=jnp.float32)
            denominator = shift - vir_ref[:, columns]
            inverse = pl.reciprocal(denominator, approx=True)
            inverse = inverse * (2.0 - denominator * inverse)
            amplitude = (integral * inverse).astype(jnp.bfloat16)
            total += lax.dot_general(
                amplitude, block, (((1,), (1,)), ((), ())), preferred_element_type=jnp.float32
            )
        for pair in range(pairs):
            contrib[pair] = jnp.transpose(total[pair * LANES : (pair + 1) * LANES])

        out_ref[:, :, my_lanes] = contrib[:, pl.ds(pl.multiple_of(me * 8, 8), 8), :]

        for_out(lambda copy: copy.start())

    swap.wait_send()
    for copy in started:
        copy.wait_send()

    for_left(lambda copy: copy.wait_send())
    mine = jnp.where(inner == idle, -1, my_tile)

    @pl.loop(0, tiles)
    def _(tile):
        @pl.when(tile != mine)
        def _():
            pltpu.make_async_remote_copy(
                src_ref=contrib.at[:, pl.ds(0, 8), :],
                dst_ref=out_ref.at[:, :, pl.ds(pl.multiple_of(tile * LANES, LANES), LANES)],
                send_sem=out_send.at[0],
                recv_sem=out_recv.at[tile],
                device_id=sibling,
                device_id_type=MESH,
            ).wait_recv()

    @pl.when(inner != idle)
    def _():
        for_out(lambda copy: copy.wait_send())


def add_pairs(left_ref, returned_ref, gamma_ref, rows, sems):
    copies = []
    for orbital in range(rows.shape[0]):
        row = jnp.where(left_ref[0] == orbital, returned_ref[0], 0.0)
        for pair in range(1, returned_ref.shape[0]):
            row += jnp.where(left_ref[pair] == orbital, returned_ref[pair], 0.0)
        rows[orbital] = row
        copies.append(pltpu.make_async_copy(rows.at[orbital], gamma_ref.at[orbital], sems.at[orbital]))
        copies[-1].start()
    for copy in copies:
        copy.wait()


def body_tiles(b_tensor, occ_energy, vir_energy, left_list, right_occ):
    occ_count, aux_rows, virtuals = b_tensor.shape
    pairs = left_list.shape[0]
    aux = 32 * aux_rows
    hbm, vmem = pl.BlockSpec(memory_space=pltpu.HBM), pl.BlockSpec(memory_space=pltpu.VMEM)
    dma = pltpu.SemaphoreType.DMA
    returned = pl.pallas_call(
        kernel,
        out_shape=jax.ShapeDtypeStruct((pairs, aux_rows, virtuals), jnp.float32),
        in_specs=[hbm] * 5,
        out_specs=vmem,
        scratch_shapes=[
            pltpu.VMEM(b_tensor.shape, jnp.bfloat16),
            pltpu.SMEM(occ_energy.shape, jnp.float32),
            pltpu.VMEM((1, virtuals), jnp.float32),
            pltpu.SMEM(left_list.shape, jnp.int32),
            pltpu.SMEM(right_occ.shape, jnp.int32),
            dma((5,)),
            pltpu.VMEM(((pairs + 1) * aux_rows, virtuals), jnp.bfloat16),
            pltpu.VMEM(((pairs + 1) * aux_rows, virtuals), jnp.bfloat16),
            pltpu.VMEM((2 * aux_rows, virtuals // 2), jnp.bfloat16),
            pltpu.VMEM((pairs, 2 * aux_rows, virtuals), jnp.bfloat16),
            pltpu.VMEM((32, 2 * aux_rows, virtuals // 2), jnp.bfloat16),
            pltpu.VMEM((pairs, aux, LANES), jnp.bfloat16),
            pltpu.VMEM((pairs * LANES, aux), jnp.bfloat16),
            pltpu.VMEM((pairs, aux, LANES), jnp.float32),
            dma, dma, dma((36,)), dma((36,)), dma((virtuals // LANES,)), dma((16,)),
            dma((32,)), dma((virtuals // LANES,)),
        ],
        compiler_params=pltpu.CompilerParams(
            collective_id=0, has_side_effects=True, vmem_limit_bytes=60 * 2**20
        ),
        cost_estimate=pl.CostEstimate(
            flops=4 * pairs * aux * virtuals * LANES, bytes_accessed=2 * occ_count * aux_rows * virtuals, transcendentals=0
        ),
    )(b_tensor, occ_energy, vir_energy.reshape(1, virtuals), left_list, right_occ)
    return pl.pallas_call(
        add_pairs,
        out_shape=jax.ShapeDtypeStruct(b_tensor.shape, jnp.float32),
        in_specs=[pl.BlockSpec(memory_space=pltpu.SMEM), vmem],
        out_specs=hbm,
        scratch_shapes=[pltpu.VMEM(b_tensor.shape, jnp.float32), dma((occ_count,))],
    )(left_list, returned)


def solution(mesh):
    placed = (P(None, ("grp", "inner"), None), P(), P(), P(), P())
    plan = body
    if mesh.shape["grp"] == 8 and mesh.shape["inner"] == 4:
        plan = body_tiles

    def program(b_tensor, *rest):
        aux, virtuals = b_tensor.shape[1:]
        fits = aux == 256 and virtuals == 3072
        return jax.shard_map(
            plan if fits else body,
            mesh=mesh,
            in_specs=placed,
            out_specs=P(None, ("grp", "inner"), None),
            check_vma=False,
        )(b_tensor, *rest)

    return program
```

```python
import jax
import jax.numpy as jnp
from jax import lax
from jax.experimental import pallas as pl
from jax.experimental.pallas import tpu as pltpu
from jax.sharding import PartitionSpec as P

MESH = pl.DeviceIdType.MESH
LANES = 128


def body(b_tensor, occ_energy, vir_energy, left_list, right_occ):
    inner_size = lax.axis_size("inner")
    group_size = lax.axis_size("grp")
    occ_count = b_tensor.shape[0]
    virtuals = b_tensor.shape[2]
    row_count = virtuals // inner_size
    col_count = virtuals // group_size
    inner_rank = lax.axis_index("inner")
    group_rank = lax.axis_index("grp")
    vir_rows = lax.dynamic_slice_in_dim(vir_energy, inner_rank * row_count, row_count)
    vir_cols = lax.dynamic_slice_in_dim(vir_energy, group_rank * col_count, col_count)
    gamma_aux = jnp.zeros(b_tensor.shape, jnp.float32)
    orbitals = jnp.arange(occ_count, dtype=jnp.int32)
    second_occ = right_occ[0]
    block_right = lax.dynamic_index_in_dim(b_tensor, second_occ, 0, keepdims=False)
    right_full = lax.all_gather(block_right, "inner", axis=0, tiled=True)
    pair_total = left_list.shape[0]
    selectors = []
    shifts = []
    partials = []
    amp_list = []
    for pair_no in range(pair_total):
        left_occ = left_list[pair_no]
        block_left = lax.dynamic_index_in_dim(b_tensor, left_occ, 0, keepdims=False)
        left_rows = lax.all_to_all(block_left, "inner", split_axis=1, concat_axis=0, tiled=True)
        partial_value = lax.dot_general(
            left_rows, right_full, (((0,), (0,)), ((), ())), preferred_element_type=jnp.float32
        )
        shift_occ = occ_energy[left_occ] + occ_energy[second_occ]
        selectors.append((orbitals == left_occ).astype(jnp.float32))
        partials.append(partial_value)
        shifts.append(shift_occ)
    stacked = jnp.stack(partials, axis=0)
    shares_all = lax.psum_scatter(stacked, "grp", scatter_dimension=2, tiled=True)
    shift_all = jnp.stack(shifts, axis=0)
    denominator_all = shift_all[:, None, None] - vir_rows[None, :, None] - vir_cols[None, None, :]
    amp_tiles = (shares_all / denominator_all).astype(jnp.bfloat16)
    amp_whole = lax.all_gather(amp_tiles, "grp", axis=2, tiled=True)
    amp_list = [amp_whole[pair_no] for pair_no in range(pair_total)]
    for pair_no in range(pair_total):
        contrib = lax.dot_general(
            right_full,
            amp_list[pair_no],
            (((1,), (1,)), ((), ())),
            preferred_element_type=jnp.float32,
        )
        returned = lax.all_to_all(contrib, "inner", split_axis=0, concat_axis=1, tiled=True)
        gamma_aux = gamma_aux + selectors[pair_no][:, None, None] * returned[None]
    return gamma_aux


def place(grp, inner):
    z, x = lax.div(grp, 2), lax.div(inner, 2)
    return z, grp - 2 * z, x, inner - 2 * x


def idle_inner(z, y):
    return 2 * lax.rem(z + y, 2) + 1


def flip_z(z, step):
    return (z, z + 1 - 2 * lax.rem(z, 2), lax.rem(z + 2, 4), 3 - z)[step]


def kernel(
    b_hbm, occ_hbm, vir_hbm, left_hbm, right_hbm, out_ref,
    b_ref, occ_ref, vir_ref, left_ref, right_ref, input_sem, own, sib, folded, pair_rows, full, left_cols, left_rows, plain, contrib,
    swap_send, swap_recv, gather_send, gather_recv, left_send, left_recv, out_send, out_recv,
):
    grp, inner = lax.axis_index("grp"), lax.axis_index("inner")
    z, y, x, core = place(grp, inner)
    me = grp * 4 + inner
    chip = grp * 2 + x
    pairs = out_ref.shape[0]
    half = full.shape[2]
    virtuals = 2 * half
    quarter = half // 2
    tiles = virtuals // LANES

    inputs = ((b_hbm, b_ref), (occ_hbm, occ_ref), (vir_hbm, vir_ref), (left_hbm, left_ref), (right_hbm, right_ref))
    fetches = [pltpu.make_async_copy(a, b, input_sem.at[n]) for n, (a, b) in enumerate(inputs)]
    for fetch in fetches:
        fetch.start()
    barrier = pltpu.get_barrier_semaphore()

    @pl.loop(0, 8)
    def _(to_grp):
        for to_inner in range(4):

            @pl.when(to_grp * 4 + to_inner != me)
            def _():
                pl.semaphore_signal(barrier, inc=1, device_id=(to_grp, to_inner), device_id_type=MESH)

    for fetch in fetches:
        fetch.wait()
    second = right_ref[0]
    folded[pl.ds(0, 8), :] = b_ref[second, :, pl.ds(0, half)]
    folded[pl.ds(8, 8), :] = b_ref[second, :, pl.ds(half, half)]
    full[me] = folded[...]
    own[pl.ds(0, 8), :] = b_ref[second]
    for pair in range(pairs):
        own[pl.ds(8 * pair + 8, 8), :] = b_ref[left_ref[pair]]
    pl.semaphore_wait(barrier, 31)

    sibling = (grp, inner + 1 - 2 * core)
    swap = pltpu.make_async_remote_copy(
        src_ref=own, dst_ref=sib, send_sem=swap_send, recv_sem=swap_recv, device_id=sibling, device_id_type=MESH
    )

    x_side = (grp, (1 - x) * 2 + core)
    y_side = (z * 2 + 1 - y, inner)
    started = []

    def send(slot, z_of, y_of, x_of, first, count, target):
        piece = full.at[(z_of * 2 + y_of) * 4 + x_of * 2 + core, :, pl.ds(first, count)]
        copy = pltpu.make_async_remote_copy(
            src_ref=piece, dst_ref=piece, send_sem=gather_send.at[slot], recv_sem=gather_recv.at[slot],
            device_id=target, device_id_type=MESH,
        )
        copy.start()
        started.append(copy)

    def arrived(slot, z_of, y_of, x_of, first, count, side=core):
        piece = full.at[(z_of * 2 + y_of) * 4 + x_of * 2 + side, :, pl.ds(first, count)]
        pltpu.make_async_remote_copy(
            src_ref=piece, dst_ref=piece, send_sem=gather_send.at[slot], recv_sem=gather_recv.at[slot],
            device_id=sibling, device_id_type=MESH,
        ).wait_recv()

    Z, X1, Y1, X2, Y2, CZ, CX, CY, CD = 0, 4, 8, 12, 16, 20, 24, 28, 32

    def spread(step):
        z_of = flip_z(z, step)
        send(X1 + step, z_of, y, x, 0, half, x_side)
        send(Y1 + step, z_of, y, x, 0, half, y_side)

    for step in (1, 2, 3):
        send(Z + step, z, y, x, 0, half, (flip_z(z, step) * 2 + y, inner))
    spread(0)
    send(CZ, z, y, x, 0, half, sibling)
    swap.start()

    def merge(low, high):
        for block in range(pairs):
            pair_rows[block, pl.ds(0, 8), :] = low[pl.ds(8 * block + 8, 8), :]
            pair_rows[block, pl.ds(8, 8), :] = high[pl.ds(8 * block + 8, 8), :]

    chip_rows = pl.ds(pl.multiple_of(chip * 16, 16), 16)

    def for_left(act):
        for side in range(2):

            @pl.when(core == side)
            def _():
                @pl.loop(0, 4)
                def _(step):
                    to_z = lax.rem(z + step, 4)
                    for to_y in range(2):
                        for slot in range(3):
                            if (to_y + slot) % 2 != side:
                                continue
                            to_grp = 2 * to_z + to_y
                            tile = 3 * to_grp + slot
                            to_inner = slot + jnp.where(slot >= idle_inner(to_z, to_y), 1, 0)
                            copy = pltpu.make_async_remote_copy(
                                src_ref=pair_rows.at[:, :, pl.ds(pl.multiple_of(tile * LANES, LANES), LANES)],
                                dst_ref=left_cols.at[:, chip_rows, :],
                                send_sem=left_send.at[tile],
                                recv_sem=left_recv.at[chip],
                                device_id=(to_grp, to_inner),
                                device_id_type=MESH,
                            )

                            @pl.when(to_grp * 2 + lax.div(to_inner, 2) != chip)
                            def _():
                                act(copy)

    def send_left():
        swap.wait_recv()

        @pl.when(core == 0)
        def _():
            merge(own, sib)

        @pl.when(core == 1)
        def _():
            merge(sib, own)

        for_left(lambda copy: copy.start())

    def relay(step):
        z_of = flip_z(z, step)
        arrived(X1 + step, z_of, y, 1 - x, 0, half)
        send(Y2 + step, z_of, y, 1 - x, 0, quarter, y_side)
        send(CX + step, z_of, y, 1 - x, 0, half, sibling)
        arrived(Y1 + step, z_of, 1 - y, x, 0, half)
        send(X2 + step, z_of, 1 - y, x, quarter, quarter, x_side)
        send(CY + step, z_of, 1 - y, x, 0, half, sibling)

    def finish(step):
        z_of = flip_z(z, step)
        arrived(Y2 + step, z_of, 1 - y, 1 - x, 0, quarter)
        arrived(X2 + step, z_of, 1 - y, 1 - x, quarter, quarter)
        send(CD + step, z_of, 1 - y, 1 - x, 0, half, sibling)

    for step in (1, 2, 3):
        z_of = flip_z(z, step)
        arrived(Z + step, z_of, y, x, 0, half)
        spread(step)
        send(CZ + step, z_of, y, x, 0, half, sibling)
        if step == 3:
            send_left()
        relay(step - 1)
        if step > 1:
            finish(step - 2)
    relay(3)
    finish(2)
    finish(3)
    for step in range(4):
        z_of = flip_z(z, step)
        arrived(CZ + step, z_of, y, x, 0, half, 1 - core)
        arrived(CX + step, z_of, y, 1 - x, 0, half, 1 - core)
        arrived(CY + step, z_of, 1 - y, x, 0, half, 1 - core)
        arrived(CD + step, z_of, 1 - y, 1 - x, 0, half, 1 - core)

    idle = idle_inner(z, y)
    my_tile = grp * 3 + inner - jnp.where(inner > idle, 1, 0)
    my_lanes = pl.ds(pl.multiple_of(my_tile * LANES, LANES), LANES)

    def for_out(act, low=0, high=pairs):
        @pl.loop(0, 8)
        def _(step):
            to_grp = lax.rem(grp + step, 8)
            for to_inner in range(4):
                other = to_grp * 4 + to_inner
                copy = pltpu.make_async_remote_copy(
                    src_ref=contrib.at[pl.ds(low, high - low), pl.ds(pl.multiple_of(other * 8, 8), 8), :],
                    dst_ref=out_ref.at[pl.ds(low, high - low), :, my_lanes],
                    send_sem=out_send.at[other],
                    recv_sem=out_recv.at[my_tile],
                    device_id=(to_grp, to_inner),
                    device_id_type=MESH,
                )

                @pl.when(other != me)
                def _():
                    act(copy)

    @pl.when(inner != idle)
    def _():
        left_cols[:, chip_rows, :] = pair_rows[:, :, my_lanes]

        @pl.loop(1, 16)
        def _(step):
            source = lax.rem(chip + step, 16)
            pltpu.make_async_remote_copy(
                src_ref=pair_rows.at[:, :, pl.ds(0, LANES)],
                dst_ref=left_cols.at[:, pl.ds(pl.multiple_of(source * 16, 16), 16), :],
                send_sem=left_send.at[0],
                recv_sem=left_recv.at[source],
                device_id=sibling,
                device_id_type=MESH,
            ).wait_recv()

        vir_cols = jnp.transpose(jnp.broadcast_to(vir_ref[:, my_lanes], (LANES, LANES)))[:, :1]
        shifts = []
        for pair in range(pairs):
            left_rows[pl.ds(pair * LANES, LANES), :] = jnp.transpose(left_cols[pair])
            shifts.append((occ_ref[left_ref[pair]] + occ_ref[second]) - vir_cols)
        wide = 4 * LANES

        def work(low, high):
            shift = jnp.concatenate(shifts[low:high], axis=0)
            left = left_rows[pl.ds(low * LANES, (high - low) * LANES), :]
            total = jnp.zeros(left.shape, jnp.float32)
            for part in range(virtuals // wide):
                columns = pl.ds(part * wide, wide)
                if low == 0:
                    side, first = divmod(part * wide, half)
                    block = full[:, pl.ds(8 * side, 8), pl.ds(first, wide)].astype(jnp.float32)
                    plain[:, columns] = block.reshape(plain.shape[0], wide).astype(jnp.bfloat16)
                block = plain[:, columns]
                integral = jnp.dot(left, block, preferred_element_type=jnp.float32)
                denominator = shift - vir_ref[:, columns]
                inverse = pl.reciprocal(denominator, approx=True)
                inverse = inverse * (2.0 - denominator * inverse)
                amplitude = (integral * inverse).astype(jnp.bfloat16)
                total += lax.dot_general(
                    amplitude, block, (((1,), (1,)), ((), ())), preferred_element_type=jnp.float32
                )
            for pair in range(low, high):
                first = (pair - low) * LANES
                contrib[pair] = jnp.transpose(total[first : first + LANES])
                out_ref[pair, :, my_lanes] = contrib[pair, pl.ds(pl.multiple_of(me * 8, 8), 8), :]
            for_out(lambda copy: copy.start(), low, high)

        work(0, 1)
        work(1, pairs)

    swap.wait_send()
    for copy in started:
        copy.wait_send()

    for_left(lambda copy: copy.wait_send())
    mine = jnp.where(inner == idle, -1, my_tile)

    @pl.loop(0, tiles)
    def _(tile):
        @pl.when(tile != mine)
        def _():
            pltpu.make_async_remote_copy(
                src_ref=contrib.at[:, pl.ds(0, 8), :],
                dst_ref=out_ref.at[:, :, pl.ds(pl.multiple_of(tile * LANES, LANES), LANES)],
                send_sem=out_send.at[0],
                recv_sem=out_recv.at[tile],
                device_id=sibling,
                device_id_type=MESH,
            ).wait_recv()

    @pl.when(inner != idle)
    def _():
        for_out(lambda copy: copy.wait_send())


def add_pairs(left_ref, returned_ref, gamma_ref, rows, sems):
    copies = []
    for orbital in range(rows.shape[0]):
        row = jnp.where(left_ref[0] == orbital, returned_ref[0], 0.0)
        for pair in range(1, returned_ref.shape[0]):
            row += jnp.where(left_ref[pair] == orbital, returned_ref[pair], 0.0)
        rows[orbital] = row
        copies.append(pltpu.make_async_copy(rows.at[orbital], gamma_ref.at[orbital], sems.at[orbital]))
        copies[-1].start()
    for copy in copies:
        copy.wait()


def body_tiles(b_tensor, occ_energy, vir_energy, left_list, right_occ):
    occ_count, aux_rows, virtuals = b_tensor.shape
    pairs = left_list.shape[0]
    aux = 32 * aux_rows
    hbm, vmem = pl.BlockSpec(memory_space=pltpu.HBM), pl.BlockSpec(memory_space=pltpu.VMEM)
    dma = pltpu.SemaphoreType.DMA
    returned = pl.pallas_call(
        kernel,
        out_shape=jax.ShapeDtypeStruct((pairs, aux_rows, virtuals), jnp.float32),
        in_specs=[hbm] * 5,
        out_specs=vmem,
        scratch_shapes=[
            pltpu.VMEM(b_tensor.shape, jnp.bfloat16),
            pltpu.SMEM(occ_energy.shape, jnp.float32),
            pltpu.VMEM((1, virtuals), jnp.float32),
            pltpu.SMEM(left_list.shape, jnp.int32),
            pltpu.SMEM(right_occ.shape, jnp.int32),
            dma((5,)),
            pltpu.VMEM(((pairs + 1) * aux_rows, virtuals), jnp.bfloat16),
            pltpu.VMEM(((pairs + 1) * aux_rows, virtuals), jnp.bfloat16),
            pltpu.VMEM((2 * aux_rows, virtuals // 2), jnp.bfloat16),
            pltpu.VMEM((pairs, 2 * aux_rows, virtuals), jnp.bfloat16),
            pltpu.VMEM((32, 2 * aux_rows, virtuals // 2), jnp.bfloat16),
            pltpu.VMEM((pairs, aux, LANES), jnp.bfloat16),
            pltpu.VMEM((pairs * LANES, aux), jnp.bfloat16),
            pltpu.VMEM((aux, virtuals), jnp.bfloat16),
            pltpu.VMEM((pairs, aux, LANES), jnp.float32),
            dma, dma, dma((36,)), dma((36,)), dma((virtuals // LANES,)), dma((16,)),
            dma((32,)), dma((virtuals // LANES,)),
        ],
        compiler_params=pltpu.CompilerParams(
            collective_id=0, has_side_effects=True, vmem_limit_bytes=60 * 2**20
        ),
        cost_estimate=pl.CostEstimate(
            flops=4 * pairs * aux * virtuals * LANES, bytes_accessed=2 * occ_count * aux_rows * virtuals, transcendentals=0
        ),
    )(b_tensor, occ_energy, vir_energy.reshape(1, virtuals), left_list, right_occ)
    return pl.pallas_call(
        add_pairs,
        out_shape=jax.ShapeDtypeStruct(b_tensor.shape, jnp.float32),
        in_specs=[pl.BlockSpec(memory_space=pltpu.SMEM), vmem],
        out_specs=hbm,
        scratch_shapes=[pltpu.VMEM(b_tensor.shape, jnp.float32), dma((occ_count,))],
    )(left_list, returned)


def solution(mesh):
    placed = (P(None, ("grp", "inner"), None), P(), P(), P(), P())
    plan = body
    if mesh.shape["grp"] == 8 and mesh.shape["inner"] == 4:
        plan = body_tiles

    def program(b_tensor, *rest):
        aux, virtuals = b_tensor.shape[1:]
        fits = aux == 256 and virtuals == 3072
        return jax.shard_map(
            plan if fits else body,
            mesh=mesh,
            in_specs=placed,
            out_specs=P(None, ("grp", "inner"), None),
            check_vma=False,
        )(b_tensor, *rest)

    return program
```

```python
import jax
import jax.numpy as jnp
from jax import lax
from jax.experimental import pallas as pl
from jax.experimental.pallas import tpu as pltpu
from jax.sharding import PartitionSpec as P

MESH = pl.DeviceIdType.MESH
LANES = 128


def body(b_tensor, occ_energy, vir_energy, left_list, right_occ):
    inner_size = lax.axis_size("inner")
    group_size = lax.axis_size("grp")
    occ_count = b_tensor.shape[0]
    virtuals = b_tensor.shape[2]
    row_count = virtuals // inner_size
    col_count = virtuals // group_size
    inner_rank = lax.axis_index("inner")
    group_rank = lax.axis_index("grp")
    vir_rows = lax.dynamic_slice_in_dim(vir_energy, inner_rank * row_count, row_count)
    vir_cols = lax.dynamic_slice_in_dim(vir_energy, group_rank * col_count, col_count)
    gamma_aux = jnp.zeros(b_tensor.shape, jnp.float32)
    orbitals = jnp.arange(occ_count, dtype=jnp.int32)
    second_occ = right_occ[0]
    block_right = lax.dynamic_index_in_dim(b_tensor, second_occ, 0, keepdims=False)
    right_full = lax.all_gather(block_right, "inner", axis=0, tiled=True)
    pair_total = left_list.shape[0]
    selectors = []
    shifts = []
    partials = []
    amp_list = []
    for pair_no in range(pair_total):
        left_occ = left_list[pair_no]
        block_left = lax.dynamic_index_in_dim(b_tensor, left_occ, 0, keepdims=False)
        left_rows = lax.all_to_all(block_left, "inner", split_axis=1, concat_axis=0, tiled=True)
        partial_value = lax.dot_general(
            left_rows, right_full, (((0,), (0,)), ((), ())), preferred_element_type=jnp.float32
        )
        shift_occ = occ_energy[left_occ] + occ_energy[second_occ]
        selectors.append((orbitals == left_occ).astype(jnp.float32))
        partials.append(partial_value)
        shifts.append(shift_occ)
    stacked = jnp.stack(partials, axis=0)
    shares_all = lax.psum_scatter(stacked, "grp", scatter_dimension=2, tiled=True)
    shift_all = jnp.stack(shifts, axis=0)
    denominator_all = shift_all[:, None, None] - vir_rows[None, :, None] - vir_cols[None, None, :]
    amp_tiles = (shares_all / denominator_all).astype(jnp.bfloat16)
    amp_whole = lax.all_gather(amp_tiles, "grp", axis=2, tiled=True)
    amp_list = [amp_whole[pair_no] for pair_no in range(pair_total)]
    for pair_no in range(pair_total):
        contrib = lax.dot_general(
            right_full,
            amp_list[pair_no],
            (((1,), (1,)), ((), ())),
            preferred_element_type=jnp.float32,
        )
        returned = lax.all_to_all(contrib, "inner", split_axis=0, concat_axis=1, tiled=True)
        gamma_aux = gamma_aux + selectors[pair_no][:, None, None] * returned[None]
    return gamma_aux


def place(grp, inner):
    z, x = lax.div(grp, 2), lax.div(inner, 2)
    return z, grp - 2 * z, x, inner - 2 * x


def idle_inner(z, y):
    return 2 * lax.rem(z + y, 2) + 1


def flip_z(z, step):
    return (z, z + 1 - 2 * lax.rem(z, 2), lax.rem(z + 2, 4), 3 - z)[step]


def kernel(
    b_hbm, occ_hbm, vir_hbm, left_hbm, right_hbm, out_ref,
    b_ref, occ_ref, vir_ref, left_ref, right_ref, input_sem, own, sib, folded, pair_rows, full, left_cols, left_rows, plain, contrib,
    swap_send, swap_recv, gather_send, gather_recv, left_send, left_recv, out_send, out_recv,
):
    grp, inner = lax.axis_index("grp"), lax.axis_index("inner")
    z, y, x, core = place(grp, inner)
    me = grp * 4 + inner
    chip = grp * 2 + x
    pairs = out_ref.shape[0]
    half = full.shape[2]
    virtuals = 2 * half
    tiles = virtuals // LANES

    inputs = ((b_hbm, b_ref), (occ_hbm, occ_ref), (vir_hbm, vir_ref), (left_hbm, left_ref), (right_hbm, right_ref))
    fetches = [pltpu.make_async_copy(a, b, input_sem.at[n]) for n, (a, b) in enumerate(inputs)]
    for fetch in fetches:
        fetch.start()
    barrier = pltpu.get_barrier_semaphore()

    @pl.loop(0, 8)
    def _(to_grp):
        for to_inner in range(4):

            @pl.when(to_grp * 4 + to_inner != me)
            def _():
                pl.semaphore_signal(barrier, inc=1, device_id=(to_grp, to_inner), device_id_type=MESH)

    for fetch in fetches:
        fetch.wait()
    second = right_ref[0]
    folded[pl.ds(0, 8), :] = b_ref[second, :, pl.ds(0, half)]
    folded[pl.ds(8, 8), :] = b_ref[second, :, pl.ds(half, half)]
    full[me] = folded[...]
    own[pl.ds(0, 8), :] = b_ref[second]
    for pair in range(pairs):
        own[pl.ds(8 * pair + 8, 8), :] = b_ref[left_ref[pair]]
    pl.semaphore_wait(barrier, 31)

    sibling = (grp, inner + 1 - 2 * core)
    swap = pltpu.make_async_remote_copy(
        src_ref=own, dst_ref=sib, send_sem=swap_send, recv_sem=swap_recv, device_id=sibling, device_id_type=MESH
    )

    x_side = (grp, (1 - x) * 2 + core)
    y_side = (z * 2 + 1 - y, inner)
    xy_side = (z * 2 + 1 - y, (1 - x) * 2 + core)
    started = []

    def send(slot, z_of, y_of, x_of, first, count, target):
        piece = full.at[(z_of * 2 + y_of) * 4 + x_of * 2 + core, :, pl.ds(first, count)]
        copy = pltpu.make_async_remote_copy(
            src_ref=piece, dst_ref=piece, send_sem=gather_send.at[slot], recv_sem=gather_recv.at[slot],
            device_id=target, device_id_type=MESH,
        )
        copy.start()
        started.append(copy)

    def arrived(slot, z_of, y_of, x_of, first, count, side=core):
        piece = full.at[(z_of * 2 + y_of) * 4 + x_of * 2 + side, :, pl.ds(first, count)]
        pltpu.make_async_remote_copy(
            src_ref=piece, dst_ref=piece, send_sem=gather_send.at[slot], recv_sem=gather_recv.at[slot],
            device_id=sibling, device_id_type=MESH,
        ).wait_recv()

    Z, X1, Y1, D1, CZ, CX, CY, CD = 0, 4, 8, 12, 16, 20, 24, 28

    def spread(step):
        z_of = flip_z(z, step)
        send(D1 + step, z_of, y, x, 0, half, xy_side)
        send(X1 + step, z_of, y, x, 0, half, x_side)
        send(Y1 + step, z_of, y, x, 0, half, y_side)

    for step in (1, 2, 3):
        send(Z + step, z, y, x, 0, half, (flip_z(z, step) * 2 + y, inner))
    spread(0)
    send(CZ, z, y, x, 0, half, sibling)
    swap.start()

    def merge(low, high):
        for block in range(pairs):
            pair_rows[block, pl.ds(0, 8), :] = low[pl.ds(8 * block + 8, 8), :]
            pair_rows[block, pl.ds(8, 8), :] = high[pl.ds(8 * block + 8, 8), :]

    chip_rows = pl.ds(pl.multiple_of(chip * 16, 16), 16)

    def for_left(act):
        for side in range(2):

            @pl.when(core == side)
            def _():
                @pl.loop(0, 4)
                def _(step):
                    to_z = lax.rem(z + step, 4)
                    for to_y in range(2):
                        for slot in range(3):
                            if (to_y + slot) % 2 != side:
                                continue
                            to_grp = 2 * to_z + to_y
                            tile = 3 * to_grp + slot
                            to_inner = slot + jnp.where(slot >= idle_inner(to_z, to_y), 1, 0)
                            copy = pltpu.make_async_remote_copy(
                                src_ref=pair_rows.at[:, :, pl.ds(pl.multiple_of(tile * LANES, LANES), LANES)],
                                dst_ref=left_cols.at[:, chip_rows, :],
                                send_sem=left_send.at[tile],
                                recv_sem=left_recv.at[chip],
                                device_id=(to_grp, to_inner),
                                device_id_type=MESH,
                            )

                            @pl.when(to_grp * 2 + lax.div(to_inner, 2) != chip)
                            def _():
                                act(copy)

    def send_left():
        swap.wait_recv()

        @pl.when(core == 0)
        def _():
            merge(own, sib)

        @pl.when(core == 1)
        def _():
            merge(sib, own)

        for_left(lambda copy: copy.start())

    def relay(step):
        z_of = flip_z(z, step)
        for slot, onward, y_of, x_of in ((X1, CX, y, 1 - x), (Y1, CY, 1 - y, x), (D1, CD, 1 - y, 1 - x)):
            arrived(slot + step, z_of, y_of, x_of, 0, half)
            send(onward + step, z_of, y_of, x_of, 0, half, sibling)

    for step in (1, 2, 3):
        z_of = flip_z(z, step)
        arrived(Z + step, z_of, y, x, 0, half)
        spread(step)
        send(CZ + step, z_of, y, x, 0, half, sibling)
        if step == 3:
            send_left()
        relay(step - 1)
    relay(3)
    for step in range(4):
        z_of = flip_z(z, step)
        arrived(CZ + step, z_of, y, x, 0, half, 1 - core)
        arrived(CX + step, z_of, y, 1 - x, 0, half, 1 - core)
        arrived(CY + step, z_of, 1 - y, x, 0, half, 1 - core)
        arrived(CD + step, z_of, 1 - y, 1 - x, 0, half, 1 - core)

    idle = idle_inner(z, y)
    my_tile = grp * 3 + inner - jnp.where(inner > idle, 1, 0)
    my_lanes = pl.ds(pl.multiple_of(my_tile * LANES, LANES), LANES)

    def for_out(act, low=0, high=pairs):
        @pl.loop(0, 8)
        def _(step):
            to_grp = lax.rem(grp + step, 8)
            for to_inner in range(4):
                other = to_grp * 4 + to_inner
                copy = pltpu.make_async_remote_copy(
                    src_ref=contrib.at[pl.ds(low, high - low), pl.ds(pl.multiple_of(other * 8, 8), 8), :],
                    dst_ref=out_ref.at[pl.ds(low, high - low), :, my_lanes],
                    send_sem=out_send.at[other],
                    recv_sem=out_recv.at[my_tile],
                    device_id=(to_grp, to_inner),
                    device_id_type=MESH,
                )

                @pl.when(other != me)
                def _():
                    act(copy)

    @pl.when(inner != idle)
    def _():
        left_cols[:, chip_rows, :] = pair_rows[:, :, my_lanes]

        @pl.loop(1, 16)
        def _(step):
            source = lax.rem(chip + step, 16)
            pltpu.make_async_remote_copy(
                src_ref=pair_rows.at[:, :, pl.ds(0, LANES)],
                dst_ref=left_cols.at[:, pl.ds(pl.multiple_of(source * 16, 16), 16), :],
                send_sem=left_send.at[0],
                recv_sem=left_recv.at[source],
                device_id=sibling,
                device_id_type=MESH,
            ).wait_recv()

        vir_cols = jnp.transpose(jnp.broadcast_to(vir_ref[:, my_lanes], (LANES, LANES)))[:, :1]
        shifts = []
        for pair in range(pairs):
            left_rows[pl.ds(pair * LANES, LANES), :] = jnp.transpose(left_cols[pair])
            shifts.append((occ_ref[left_ref[pair]] + occ_ref[second]) - vir_cols)
        wide = 4 * LANES

        def work(low, high):
            shift = jnp.concatenate(shifts[low:high], axis=0)
            left = left_rows[pl.ds(low * LANES, (high - low) * LANES), :]
            total = jnp.zeros(left.shape, jnp.float32)
            for part in range(virtuals // wide):
                columns = pl.ds(part * wide, wide)
                if low == 0:
                    side, first = divmod(part * wide, half)
                    block = full[:, pl.ds(8 * side, 8), pl.ds(first, wide)].astype(jnp.float32)
                    plain[:, columns] = block.reshape(plain.shape[0], wide).astype(jnp.bfloat16)
                block = plain[:, columns]
                integral = jnp.dot(left, block, preferred_element_type=jnp.float32)
                denominator = shift - vir_ref[:, columns]
                inverse = pl.reciprocal(denominator, approx=True)
                inverse = inverse * (2.0 - denominator * inverse)
                amplitude = (integral * inverse).astype(jnp.bfloat16)
                total += lax.dot_general(
                    amplitude, block, (((1,), (1,)), ((), ())), preferred_element_type=jnp.float32
                )
            for pair in range(low, high):
                first = (pair - low) * LANES
                contrib[pair] = jnp.transpose(total[first : first + LANES])
                out_ref[pair, :, my_lanes] = contrib[pair, pl.ds(pl.multiple_of(me * 8, 8), 8), :]
            for_out(lambda copy: copy.start(), low, high)

        work(0, 1)
        work(1, pairs)

    swap.wait_send()
    for copy in started:
        copy.wait_send()

    for_left(lambda copy: copy.wait_send())
    mine = jnp.where(inner == idle, -1, my_tile)

    @pl.loop(0, tiles)
    def _(tile):
        @pl.when(tile != mine)
        def _():
            pltpu.make_async_remote_copy(
                src_ref=contrib.at[:, pl.ds(0, 8), :],
                dst_ref=out_ref.at[:, :, pl.ds(pl.multiple_of(tile * LANES, LANES), LANES)],
                send_sem=out_send.at[0],
                recv_sem=out_recv.at[tile],
                device_id=sibling,
                device_id_type=MESH,
            ).wait_recv()

    @pl.when(inner != idle)
    def _():
        for_out(lambda copy: copy.wait_send())


def add_pairs(left_ref, returned_ref, gamma_ref, rows, sems):
    copies = []
    for orbital in range(rows.shape[0]):
        row = jnp.where(left_ref[0] == orbital, returned_ref[0], 0.0)
        for pair in range(1, returned_ref.shape[0]):
            row += jnp.where(left_ref[pair] == orbital, returned_ref[pair], 0.0)
        rows[orbital] = row
        copies.append(pltpu.make_async_copy(rows.at[orbital], gamma_ref.at[orbital], sems.at[orbital]))
        copies[-1].start()
    for copy in copies:
        copy.wait()


def body_tiles(b_tensor, occ_energy, vir_energy, left_list, right_occ):
    occ_count, aux_rows, virtuals = b_tensor.shape
    pairs = left_list.shape[0]
    aux = 32 * aux_rows
    hbm, vmem = pl.BlockSpec(memory_space=pltpu.HBM), pl.BlockSpec(memory_space=pltpu.VMEM)
    dma = pltpu.SemaphoreType.DMA
    returned = pl.pallas_call(
        kernel,
        out_shape=jax.ShapeDtypeStruct((pairs, aux_rows, virtuals), jnp.float32),
        in_specs=[hbm] * 5,
        out_specs=vmem,
        scratch_shapes=[
            pltpu.VMEM(b_tensor.shape, jnp.bfloat16),
            pltpu.SMEM(occ_energy.shape, jnp.float32),
            pltpu.VMEM((1, virtuals), jnp.float32),
            pltpu.SMEM(left_list.shape, jnp.int32),
            pltpu.SMEM(right_occ.shape, jnp.int32),
            dma((5,)),
            pltpu.VMEM(((pairs + 1) * aux_rows, virtuals), jnp.bfloat16),
            pltpu.VMEM(((pairs + 1) * aux_rows, virtuals), jnp.bfloat16),
            pltpu.VMEM((2 * aux_rows, virtuals // 2), jnp.bfloat16),
            pltpu.VMEM((pairs, 2 * aux_rows, virtuals), jnp.bfloat16),
            pltpu.VMEM((32, 2 * aux_rows, virtuals // 2), jnp.bfloat16),
            pltpu.VMEM((pairs, aux, LANES), jnp.bfloat16),
            pltpu.VMEM((pairs * LANES, aux), jnp.bfloat16),
            pltpu.VMEM((aux, virtuals), jnp.bfloat16),
            pltpu.VMEM((pairs, aux, LANES), jnp.float32),
            dma, dma, dma((32,)), dma((32,)), dma((virtuals // LANES,)), dma((16,)),
            dma((32,)), dma((virtuals // LANES,)),
        ],
        compiler_params=pltpu.CompilerParams(
            collective_id=0, has_side_effects=True, vmem_limit_bytes=60 * 2**20
        ),
        cost_estimate=pl.CostEstimate(
            flops=4 * pairs * aux * virtuals * LANES, bytes_accessed=2 * occ_count * aux_rows * virtuals, transcendentals=0
        ),
    )(b_tensor, occ_energy, vir_energy.reshape(1, virtuals), left_list, right_occ)
    return pl.pallas_call(
        add_pairs,
        out_shape=jax.ShapeDtypeStruct(b_tensor.shape, jnp.float32),
        in_specs=[pl.BlockSpec(memory_space=pltpu.SMEM), vmem],
        out_specs=hbm,
        scratch_shapes=[pltpu.VMEM(b_tensor.shape, jnp.float32), dma((occ_count,))],
    )(left_list, returned)


def solution(mesh):
    placed = (P(None, ("grp", "inner"), None), P(), P(), P(), P())
    plan = body
    if mesh.shape["grp"] == 8 and mesh.shape["inner"] == 4:
        plan = body_tiles

    def program(b_tensor, *rest):
        aux, virtuals = b_tensor.shape[1:]
        fits = aux == 256 and virtuals == 3072
        return jax.shard_map(
            plan if fits else body,
            mesh=mesh,
            in_specs=placed,
            out_specs=P(None, ("grp", "inner"), None),
            check_vma=False,
        )(b_tensor, *rest)

    return program
```

```python
import jax
import jax.numpy as jnp
from jax import lax
from jax.experimental import pallas as pl
from jax.experimental.pallas import tpu as pltpu
from jax.sharding import PartitionSpec as P

MESH = pl.DeviceIdType.MESH
LANES = 128


def body(b_tensor, occ_energy, vir_energy, left_list, right_occ):
    inner_size = lax.axis_size("inner")
    group_size = lax.axis_size("grp")
    occ_count = b_tensor.shape[0]
    virtuals = b_tensor.shape[2]
    row_count = virtuals // inner_size
    col_count = virtuals // group_size
    inner_rank = lax.axis_index("inner")
    group_rank = lax.axis_index("grp")
    vir_rows = lax.dynamic_slice_in_dim(vir_energy, inner_rank * row_count, row_count)
    vir_cols = lax.dynamic_slice_in_dim(vir_energy, group_rank * col_count, col_count)
    gamma_aux = jnp.zeros(b_tensor.shape, jnp.float32)
    orbitals = jnp.arange(occ_count, dtype=jnp.int32)
    second_occ = right_occ[0]
    block_right = lax.dynamic_index_in_dim(b_tensor, second_occ, 0, keepdims=False)
    right_full = lax.all_gather(block_right, "inner", axis=0, tiled=True)
    pair_total = left_list.shape[0]
    selectors = []
    shifts = []
    partials = []
    amp_list = []
    for pair_no in range(pair_total):
        left_occ = left_list[pair_no]
        block_left = lax.dynamic_index_in_dim(b_tensor, left_occ, 0, keepdims=False)
        left_rows = lax.all_to_all(block_left, "inner", split_axis=1, concat_axis=0, tiled=True)
        partial_value = lax.dot_general(
            left_rows, right_full, (((0,), (0,)), ((), ())), preferred_element_type=jnp.float32
        )
        shift_occ = occ_energy[left_occ] + occ_energy[second_occ]
        selectors.append((orbitals == left_occ).astype(jnp.float32))
        partials.append(partial_value)
        shifts.append(shift_occ)
    stacked = jnp.stack(partials, axis=0)
    shares_all = lax.psum_scatter(stacked, "grp", scatter_dimension=2, tiled=True)
    shift_all = jnp.stack(shifts, axis=0)
    denominator_all = shift_all[:, None, None] - vir_rows[None, :, None] - vir_cols[None, None, :]
    amp_tiles = (shares_all / denominator_all).astype(jnp.bfloat16)
    amp_whole = lax.all_gather(amp_tiles, "grp", axis=2, tiled=True)
    amp_list = [amp_whole[pair_no] for pair_no in range(pair_total)]
    for pair_no in range(pair_total):
        contrib = lax.dot_general(
            right_full,
            amp_list[pair_no],
            (((1,), (1,)), ((), ())),
            preferred_element_type=jnp.float32,
        )
        returned = lax.all_to_all(contrib, "inner", split_axis=0, concat_axis=1, tiled=True)
        gamma_aux = gamma_aux + selectors[pair_no][:, None, None] * returned[None]
    return gamma_aux


def place(grp, inner):
    z, x = lax.div(grp, 2), lax.div(inner, 2)
    return z, grp - 2 * z, x, inner - 2 * x


def idle_inner(z, y):
    return 2 * lax.rem(z + y, 2) + 1


def flip_z(z, step):
    return (z, z + 1 - 2 * lax.rem(z, 2), lax.rem(z + 2, 4), 3 - z)[step]


def kernel(
    b_hbm, occ_hbm, vir_hbm, left_hbm, right_hbm, out_ref,
    b_ref, occ_ref, vir_ref, left_ref, right_ref, input_sem, own, sib, folded, pair_rows, full, left_cols, left_rows, plain, contrib,
    swap_send, swap_recv, gather_send, gather_recv, left_send, left_recv, out_send, out_recv,
):
    grp, inner = lax.axis_index("grp"), lax.axis_index("inner")
    z, y, x, core = place(grp, inner)
    me = grp * 4 + inner
    chip = grp * 2 + x
    pairs = out_ref.shape[0]
    half = full.shape[2]
    virtuals = 2 * half
    tiles = virtuals // LANES

    inputs = ((b_hbm, b_ref), (occ_hbm, occ_ref), (vir_hbm, vir_ref), (left_hbm, left_ref), (right_hbm, right_ref))
    fetches = [pltpu.make_async_copy(a, b, input_sem.at[n]) for n, (a, b) in enumerate(inputs)]
    for fetch in fetches:
        fetch.start()
    barrier = pltpu.get_barrier_semaphore()

    @pl.loop(0, 8)
    def _(to_grp):
        for to_inner in range(4):

            @pl.when(to_grp * 4 + to_inner != me)
            def _():
                pl.semaphore_signal(barrier, inc=1, device_id=(to_grp, to_inner), device_id_type=MESH)

    for fetch in fetches:
        fetch.wait()
    second = right_ref[0]
    folded[pl.ds(0, 8), :] = b_ref[second, :, pl.ds(0, half)]
    folded[pl.ds(8, 8), :] = b_ref[second, :, pl.ds(half, half)]
    full[me] = folded[...]
    own[pl.ds(0, 8), :] = b_ref[second]
    for pair in range(pairs):
        own[pl.ds(8 * pair + 8, 8), :] = b_ref[left_ref[pair]]
    pl.semaphore_wait(barrier, 31)

    sibling = (grp, inner + 1 - 2 * core)
    swap = pltpu.make_async_remote_copy(
        src_ref=own, dst_ref=sib, send_sem=swap_send, recv_sem=swap_recv, device_id=sibling, device_id_type=MESH
    )

    x_side = (grp, (1 - x) * 2 + core)
    y_side = (z * 2 + 1 - y, inner)
    xy_side = (z * 2 + 1 - y, (1 - x) * 2 + core)
    started = []

    def send(slot, z_of, y_of, x_of, first, count, target):
        piece = full.at[(z_of * 2 + y_of) * 4 + x_of * 2 + core, :, pl.ds(first, count)]
        copy = pltpu.make_async_remote_copy(
            src_ref=piece, dst_ref=piece, send_sem=gather_send.at[slot], recv_sem=gather_recv.at[slot],
            device_id=target, device_id_type=MESH,
        )
        copy.start()
        started.append(copy)

    def arrived(slot, z_of, y_of, x_of, first, count, side=core):
        piece = full.at[(z_of * 2 + y_of) * 4 + x_of * 2 + side, :, pl.ds(first, count)]
        pltpu.make_async_remote_copy(
            src_ref=piece, dst_ref=piece, send_sem=gather_send.at[slot], recv_sem=gather_recv.at[slot],
            device_id=sibling, device_id_type=MESH,
        ).wait_recv()

    Z, X1, Y1, D1, CZ, CX, CY, CD = 0, 4, 8, 12, 16, 20, 24, 28

    def spread(step):
        z_of = flip_z(z, step)
        send(D1 + step, z_of, y, x, 0, half, xy_side)
        send(X1 + step, z_of, y, x, 0, half, x_side)
        send(Y1 + step, z_of, y, x, 0, half, y_side)

    for step in (1, 2, 3):
        send(Z + step, z, y, x, 0, half, (flip_z(z, step) * 2 + y, inner))
    spread(0)
    send(CZ, z, y, x, 0, half, sibling)
    swap.start()

    def merge(low, high):
        for block in range(pairs):
            pair_rows[block, pl.ds(0, 8), :] = low[pl.ds(8 * block + 8, 8), :]
            pair_rows[block, pl.ds(8, 8), :] = high[pl.ds(8 * block + 8, 8), :]

    chip_rows = pl.ds(pl.multiple_of(chip * 16, 16), 16)

    def for_left(act):
        for side in range(2):

            @pl.when(core == side)
            def _():
                @pl.loop(0, 4)
                def _(step):
                    to_z = lax.rem(z + step, 4)
                    for to_y in range(2):
                        for slot in range(3):
                            if (to_y + slot) % 2 != side:
                                continue
                            to_grp = 2 * to_z + to_y
                            tile = 3 * to_grp + slot
                            to_inner = slot + jnp.where(slot >= idle_inner(to_z, to_y), 1, 0)
                            copy = pltpu.make_async_remote_copy(
                                src_ref=pair_rows.at[:, :, pl.ds(pl.multiple_of(tile * LANES, LANES), LANES)],
                                dst_ref=left_cols.at[:, chip_rows, :],
                                send_sem=left_send.at[tile],
                                recv_sem=left_recv.at[chip],
                                device_id=(to_grp, to_inner),
                                device_id_type=MESH,
                            )

                            @pl.when(to_grp * 2 + lax.div(to_inner, 2) != chip)
                            def _():
                                act(copy)

    def send_left():
        swap.wait_recv()

        @pl.when(core == 0)
        def _():
            merge(own, sib)

        @pl.when(core == 1)
        def _():
            merge(sib, own)

        for_left(lambda copy: copy.start())

    def relay(step):
        z_of = flip_z(z, step)
        for slot, onward, y_of, x_of in ((X1, CX, y, 1 - x), (Y1, CY, 1 - y, x), (D1, CD, 1 - y, 1 - x)):
            arrived(slot + step, z_of, y_of, x_of, 0, half)
            send(onward + step, z_of, y_of, x_of, 0, half, sibling)

    for step in (1, 2, 3):
        z_of = flip_z(z, step)
        arrived(Z + step, z_of, y, x, 0, half)
        spread(step)
        send(CZ + step, z_of, y, x, 0, half, sibling)
        if step == 3:
            send_left()
        relay(step - 1)
    relay(3)
    for step in range(4):
        z_of = flip_z(z, step)
        arrived(CZ + step, z_of, y, x, 0, half, 1 - core)
        arrived(CX + step, z_of, y, 1 - x, 0, half, 1 - core)
        arrived(CY + step, z_of, 1 - y, x, 0, half, 1 - core)
        arrived(CD + step, z_of, 1 - y, 1 - x, 0, half, 1 - core)

    idle = idle_inner(z, y)
    my_tile = grp * 3 + inner - jnp.where(inner > idle, 1, 0)
    my_lanes = pl.ds(pl.multiple_of(my_tile * LANES, LANES), LANES)

    def for_out(act, low=0, high=pairs):
        @pl.loop(0, 8)
        def _(step):
            to_grp = lax.rem(grp + 4 + step, 8)
            for to_inner in range(4):
                other = to_grp * 4 + to_inner
                copy = pltpu.make_async_remote_copy(
                    src_ref=contrib.at[pl.ds(low, high - low), pl.ds(pl.multiple_of(other * 8, 8), 8), :],
                    dst_ref=out_ref.at[pl.ds(low, high - low), :, my_lanes],
                    send_sem=out_send.at[other],
                    recv_sem=out_recv.at[my_tile],
                    device_id=(to_grp, to_inner),
                    device_id_type=MESH,
                )

                @pl.when(other != me)
                def _():
                    act(copy)

    @pl.when(inner != idle)
    def _():
        left_cols[:, chip_rows, :] = pair_rows[:, :, my_lanes]

        @pl.loop(1, 16)
        def _(step):
            source = lax.rem(chip + step, 16)
            pltpu.make_async_remote_copy(
                src_ref=pair_rows.at[:, :, pl.ds(0, LANES)],
                dst_ref=left_cols.at[:, pl.ds(pl.multiple_of(source * 16, 16), 16), :],
                send_sem=left_send.at[0],
                recv_sem=left_recv.at[source],
                device_id=sibling,
                device_id_type=MESH,
            ).wait_recv()

        vir_cols = jnp.transpose(jnp.broadcast_to(vir_ref[:, my_lanes], (LANES, LANES)))[:, :1]
        shifts = []
        for pair in range(pairs):
            left_rows[pl.ds(pair * LANES, LANES), :] = jnp.transpose(left_cols[pair])
            shifts.append((occ_ref[left_ref[pair]] + occ_ref[second]) - vir_cols)
        wide = 4 * LANES

        def work(low, high):
            shift = jnp.concatenate(shifts[low:high], axis=0)
            left = left_rows[pl.ds(low * LANES, (high - low) * LANES), :]
            total = jnp.zeros(left.shape, jnp.float32)
            for part in range(virtuals // wide):
                columns = pl.ds(part * wide, wide)
                if low == 0:
                    side, first = divmod(part * wide, half)
                    block = full[:, pl.ds(8 * side, 8), pl.ds(first, wide)].astype(jnp.float32)
                    plain[:, columns] = block.reshape(plain.shape[0], wide).astype(jnp.bfloat16)
                block = plain[:, columns]
                integral = jnp.dot(left, block, preferred_element_type=jnp.float32)
                denominator = shift - vir_ref[:, columns]
                inverse = pl.reciprocal(denominator, approx=True)
                inverse = inverse * (2.0 - denominator * inverse)
                amplitude = (integral * inverse).astype(jnp.bfloat16)
                total += lax.dot_general(
                    amplitude, block, (((1,), (1,)), ((), ())), preferred_element_type=jnp.float32
                )
            for pair in range(low, high):
                first = (pair - low) * LANES
                contrib[pair] = jnp.transpose(total[first : first + LANES])
                out_ref[pair, :, my_lanes] = contrib[pair, pl.ds(pl.multiple_of(me * 8, 8), 8), :]
            for_out(lambda copy: copy.start(), low, high)

        work(0, 1)
        work(1, pairs)

    swap.wait_send()
    for copy in started:
        copy.wait_send()

    for_left(lambda copy: copy.wait_send())
    mine = jnp.where(inner == idle, -1, my_tile)

    @pl.loop(0, tiles)
    def _(tile):
        @pl.when(tile != mine)
        def _():
            pltpu.make_async_remote_copy(
                src_ref=contrib.at[:, pl.ds(0, 8), :],
                dst_ref=out_ref.at[:, :, pl.ds(pl.multiple_of(tile * LANES, LANES), LANES)],
                send_sem=out_send.at[0],
                recv_sem=out_recv.at[tile],
                device_id=sibling,
                device_id_type=MESH,
            ).wait_recv()

    @pl.when(inner != idle)
    def _():
        for_out(lambda copy: copy.wait_send())


def add_pairs(left_ref, returned_ref, gamma_ref, rows, sems):
    copies = []
    for orbital in range(rows.shape[0]):
        row = jnp.where(left_ref[0] == orbital, returned_ref[0], 0.0)
        for pair in range(1, returned_ref.shape[0]):
            row += jnp.where(left_ref[pair] == orbital, returned_ref[pair], 0.0)
        rows[orbital] = row
        copies.append(pltpu.make_async_copy(rows.at[orbital], gamma_ref.at[orbital], sems.at[orbital]))
        copies[-1].start()
    for copy in copies:
        copy.wait()


def body_tiles(b_tensor, occ_energy, vir_energy, left_list, right_occ):
    occ_count, aux_rows, virtuals = b_tensor.shape
    pairs = left_list.shape[0]
    aux = 32 * aux_rows
    hbm, vmem = pl.BlockSpec(memory_space=pltpu.HBM), pl.BlockSpec(memory_space=pltpu.VMEM)
    dma = pltpu.SemaphoreType.DMA
    returned = pl.pallas_call(
        kernel,
        out_shape=jax.ShapeDtypeStruct((pairs, aux_rows, virtuals), jnp.float32),
        in_specs=[hbm] * 5,
        out_specs=vmem,
        scratch_shapes=[
            pltpu.VMEM(b_tensor.shape, jnp.bfloat16),
            pltpu.SMEM(occ_energy.shape, jnp.float32),
            pltpu.VMEM((1, virtuals), jnp.float32),
            pltpu.SMEM(left_list.shape, jnp.int32),
            pltpu.SMEM(right_occ.shape, jnp.int32),
            dma((5,)),
            pltpu.VMEM(((pairs + 1) * aux_rows, virtuals), jnp.bfloat16),
            pltpu.VMEM(((pairs + 1) * aux_rows, virtuals), jnp.bfloat16),
            pltpu.VMEM((2 * aux_rows, virtuals // 2), jnp.bfloat16),
            pltpu.VMEM((pairs, 2 * aux_rows, virtuals), jnp.bfloat16),
            pltpu.VMEM((32, 2 * aux_rows, virtuals // 2), jnp.bfloat16),
            pltpu.VMEM((pairs, aux, LANES), jnp.bfloat16),
            pltpu.VMEM((pairs * LANES, aux), jnp.bfloat16),
            pltpu.VMEM((aux, virtuals), jnp.bfloat16),
            pltpu.VMEM((pairs, aux, LANES), jnp.float32),
            dma, dma, dma((32,)), dma((32,)), dma((virtuals // LANES,)), dma((16,)),
            dma((32,)), dma((virtuals // LANES,)),
        ],
        compiler_params=pltpu.CompilerParams(
            collective_id=0, has_side_effects=True, vmem_limit_bytes=60 * 2**20
        ),
        cost_estimate=pl.CostEstimate(
            flops=4 * pairs * aux * virtuals * LANES, bytes_accessed=2 * occ_count * aux_rows * virtuals, transcendentals=0
        ),
    )(b_tensor, occ_energy, vir_energy.reshape(1, virtuals), left_list, right_occ)
    return pl.pallas_call(
        add_pairs,
        out_shape=jax.ShapeDtypeStruct(b_tensor.shape, jnp.float32),
        in_specs=[pl.BlockSpec(memory_space=pltpu.SMEM), vmem],
        out_specs=hbm,
        scratch_shapes=[pltpu.VMEM(b_tensor.shape, jnp.float32), dma((occ_count,))],
    )(left_list, returned)


def solution(mesh):
    placed = (P(None, ("grp", "inner"), None), P(), P(), P(), P())
    plan = body
    if mesh.shape["grp"] == 8 and mesh.shape["inner"] == 4:
        plan = body_tiles

    def program(b_tensor, *rest):
        aux, virtuals = b_tensor.shape[1:]
        fits = aux == 256 and virtuals == 3072
        return jax.shard_map(
            plan if fits else body,
            mesh=mesh,
            in_specs=placed,
            out_specs=P(None, ("grp", "inner"), None),
            check_vma=False,
        )(b_tensor, *rest)

    return program
```

```python
import jax
import jax.numpy as jnp
from jax import lax
from jax.experimental import pallas as pl
from jax.experimental.pallas import tpu as pltpu
from jax.sharding import PartitionSpec as P

MESH = pl.DeviceIdType.MESH
LANES = 128


def body(b_tensor, occ_energy, vir_energy, left_list, right_occ):
    inner_size = lax.axis_size("inner")
    group_size = lax.axis_size("grp")
    occ_count = b_tensor.shape[0]
    virtuals = b_tensor.shape[2]
    row_count = virtuals // inner_size
    col_count = virtuals // group_size
    inner_rank = lax.axis_index("inner")
    group_rank = lax.axis_index("grp")
    vir_rows = lax.dynamic_slice_in_dim(vir_energy, inner_rank * row_count, row_count)
    vir_cols = lax.dynamic_slice_in_dim(vir_energy, group_rank * col_count, col_count)
    gamma_aux = jnp.zeros(b_tensor.shape, jnp.float32)
    orbitals = jnp.arange(occ_count, dtype=jnp.int32)
    second_occ = right_occ[0]
    block_right = lax.dynamic_index_in_dim(b_tensor, second_occ, 0, keepdims=False)
    right_full = lax.all_gather(block_right, "inner", axis=0, tiled=True)
    pair_total = left_list.shape[0]
    selectors = []
    shifts = []
    partials = []
    amp_list = []
    for pair_no in range(pair_total):
        left_occ = left_list[pair_no]
        block_left = lax.dynamic_index_in_dim(b_tensor, left_occ, 0, keepdims=False)
        left_rows = lax.all_to_all(block_left, "inner", split_axis=1, concat_axis=0, tiled=True)
        partial_value = lax.dot_general(
            left_rows, right_full, (((0,), (0,)), ((), ())), preferred_element_type=jnp.float32
        )
        shift_occ = occ_energy[left_occ] + occ_energy[second_occ]
        selectors.append((orbitals == left_occ).astype(jnp.float32))
        partials.append(partial_value)
        shifts.append(shift_occ)
    stacked = jnp.stack(partials, axis=0)
    shares_all = lax.psum_scatter(stacked, "grp", scatter_dimension=2, tiled=True)
    shift_all = jnp.stack(shifts, axis=0)
    denominator_all = shift_all[:, None, None] - vir_rows[None, :, None] - vir_cols[None, None, :]
    amp_tiles = (shares_all / denominator_all).astype(jnp.bfloat16)
    amp_whole = lax.all_gather(amp_tiles, "grp", axis=2, tiled=True)
    amp_list = [amp_whole[pair_no] for pair_no in range(pair_total)]
    for pair_no in range(pair_total):
        contrib = lax.dot_general(
            right_full,
            amp_list[pair_no],
            (((1,), (1,)), ((), ())),
            preferred_element_type=jnp.float32,
        )
        returned = lax.all_to_all(contrib, "inner", split_axis=0, concat_axis=1, tiled=True)
        gamma_aux = gamma_aux + selectors[pair_no][:, None, None] * returned[None]
    return gamma_aux


def place(grp, inner):
    z, x = lax.div(grp, 2), lax.div(inner, 2)
    return z, grp - 2 * z, x, inner - 2 * x


def idle_inner(z, y):
    return 2 * lax.rem(z + y, 2) + 1


def flip_z(z, step):
    return (z, z + 1 - 2 * lax.rem(z, 2), lax.rem(z + 2, 4), 3 - z)[step]


def kernel(
    b_hbm, occ_hbm, vir_hbm, left_hbm, right_hbm, out_ref,
    b_ref, occ_ref, vir_ref, left_ref, right_ref, input_sem, own, sib, folded, pair_rows, full, left_cols, left_rows, plain, contrib,
    swap_send, swap_recv, gather_send, gather_recv, left_send, left_recv, out_send, out_recv,
):
    grp, inner = lax.axis_index("grp"), lax.axis_index("inner")
    z, y, x, core = place(grp, inner)
    me = grp * 4 + inner
    chip = grp * 2 + x
    pairs = out_ref.shape[0]
    half = full.shape[2]
    virtuals = 2 * half
    tiles = virtuals // LANES

    inputs = ((b_hbm, b_ref), (occ_hbm, occ_ref), (vir_hbm, vir_ref), (left_hbm, left_ref), (right_hbm, right_ref))
    fetches = [pltpu.make_async_copy(a, b, input_sem.at[n]) for n, (a, b) in enumerate(inputs)]
    for fetch in fetches:
        fetch.start()
    barrier = pltpu.get_barrier_semaphore()

    @pl.loop(0, 8)
    def _(to_grp):
        for to_inner in range(4):

            @pl.when(to_grp * 4 + to_inner != me)
            def _():
                pl.semaphore_signal(barrier, inc=1, device_id=(to_grp, to_inner), device_id_type=MESH)

    for fetch in fetches:
        fetch.wait()
    second = right_ref[0]
    folded[pl.ds(0, 8), :] = b_ref[second, :, pl.ds(0, half)]
    folded[pl.ds(8, 8), :] = b_ref[second, :, pl.ds(half, half)]
    full[me] = folded[...]
    own[pl.ds(0, 8), :] = b_ref[second]
    for pair in range(pairs):
        own[pl.ds(8 * pair + 8, 8), :] = b_ref[left_ref[pair]]
    pl.semaphore_wait(barrier, 31)

    sibling = (grp, inner + 1 - 2 * core)
    swap = pltpu.make_async_remote_copy(
        src_ref=own, dst_ref=sib, send_sem=swap_send, recv_sem=swap_recv, device_id=sibling, device_id_type=MESH
    )

    x_side = (grp, (1 - x) * 2 + core)
    y_side = (z * 2 + 1 - y, inner)
    xy_side = (z * 2 + 1 - y, (1 - x) * 2 + core)
    started = []

    def send(slot, z_of, y_of, x_of, first, count, target):
        piece = full.at[(z_of * 2 + y_of) * 4 + x_of * 2 + core, :, pl.ds(first, count)]
        copy = pltpu.make_async_remote_copy(
            src_ref=piece, dst_ref=piece, send_sem=gather_send.at[slot], recv_sem=gather_recv.at[slot],
            device_id=target, device_id_type=MESH,
        )
        copy.start()
        started.append(copy)

    def arrived(slot, z_of, y_of, x_of, first, count, side=core):
        piece = full.at[(z_of * 2 + y_of) * 4 + x_of * 2 + side, :, pl.ds(first, count)]
        pltpu.make_async_remote_copy(
            src_ref=piece, dst_ref=piece, send_sem=gather_send.at[slot], recv_sem=gather_recv.at[slot],
            device_id=sibling, device_id_type=MESH,
        ).wait_recv()

    Z, X1, Y1, D1, CZ, CX, CY, CD = 0, 4, 8, 12, 16, 20, 24, 28

    def spread(step):
        z_of = flip_z(z, step)
        send(X1 + step, z_of, y, x, 0, half, x_side)
        send(Y1 + step, z_of, y, x, 0, half, y_side)
        send(D1 + step, z_of, y, x, 0, half, xy_side)

    for step in (1, 2, 3):
        send(Z + step, z, y, x, 0, half, (flip_z(z, step) * 2 + y, inner))
    spread(0)
    send(CZ, z, y, x, 0, half, sibling)
    swap.start()

    def merge(low, high):
        for block in range(pairs):
            pair_rows[block, pl.ds(0, 8), :] = low[pl.ds(8 * block + 8, 8), :]
            pair_rows[block, pl.ds(8, 8), :] = high[pl.ds(8 * block + 8, 8), :]

    chip_rows = pl.ds(pl.multiple_of(chip * 16, 16), 16)

    def for_left(act):
        for side in range(2):

            @pl.when(core == side)
            def _():
                @pl.loop(0, 4)
                def _(step):
                    to_z = lax.rem(z + step, 4)
                    for to_y in range(2):
                        for slot in range(3):
                            if (to_y + slot) % 2 != side:
                                continue
                            to_grp = 2 * to_z + to_y
                            tile = 3 * to_grp + slot
                            to_inner = slot + jnp.where(slot >= idle_inner(to_z, to_y), 1, 0)
                            copy = pltpu.make_async_remote_copy(
                                src_ref=pair_rows.at[:, :, pl.ds(pl.multiple_of(tile * LANES, LANES), LANES)],
                                dst_ref=left_cols.at[:, chip_rows, :],
                                send_sem=left_send.at[tile],
                                recv_sem=left_recv.at[chip],
                                device_id=(to_grp, to_inner),
                                device_id_type=MESH,
                            )

                            @pl.when(to_grp * 2 + lax.div(to_inner, 2) != chip)
                            def _():
                                act(copy)

    def send_left():
        swap.wait_recv()

        @pl.when(core == 0)
        def _():
            merge(own, sib)

        @pl.when(core == 1)
        def _():
            merge(sib, own)

        for_left(lambda copy: copy.start())

    def relay(step):
        z_of = flip_z(z, step)
        for slot, onward, y_of, x_of in ((X1, CX, y, 1 - x), (Y1, CY, 1 - y, x), (D1, CD, 1 - y, 1 - x)):
            arrived(slot + step, z_of, y_of, x_of, 0, half)
            send(onward + step, z_of, y_of, x_of, 0, half, sibling)

    for step in (1, 2, 3):
        z_of = flip_z(z, step)
        arrived(Z + step, z_of, y, x, 0, half)
        spread(step)
        send(CZ + step, z_of, y, x, 0, half, sibling)
        if step == 3:
            send_left()
        relay(step - 1)
    relay(3)
    for step in range(4):
        z_of = flip_z(z, step)
        arrived(CZ + step, z_of, y, x, 0, half, 1 - core)
        arrived(CX + step, z_of, y, 1 - x, 0, half, 1 - core)
        arrived(CY + step, z_of, 1 - y, x, 0, half, 1 - core)
        arrived(CD + step, z_of, 1 - y, 1 - x, 0, half, 1 - core)

    idle = idle_inner(z, y)
    my_tile = grp * 3 + inner - jnp.where(inner > idle, 1, 0)
    my_lanes = pl.ds(pl.multiple_of(my_tile * LANES, LANES), LANES)

    def for_out(act, low=0, high=pairs):
        @pl.loop(0, 8)
        def _(step):
            to_grp = lax.rem(grp + step, 8)
            for to_inner in range(4):
                other = to_grp * 4 + to_inner
                copy = pltpu.make_async_remote_copy(
                    src_ref=contrib.at[pl.ds(low, high - low), pl.ds(pl.multiple_of(other * 8, 8), 8), :],
                    dst_ref=out_ref.at[pl.ds(low, high - low), :, my_lanes],
                    send_sem=out_send.at[other],
                    recv_sem=out_recv.at[my_tile],
                    device_id=(to_grp, to_inner),
                    device_id_type=MESH,
                )

                @pl.when(other != me)
                def _():
                    act(copy)

    @pl.when(inner != idle)
    def _():
        left_cols[:, chip_rows, :] = pair_rows[:, :, my_lanes]

        @pl.loop(1, 16)
        def _(step):
            source = lax.rem(chip + step, 16)
            pltpu.make_async_remote_copy(
                src_ref=pair_rows.at[:, :, pl.ds(0, LANES)],
                dst_ref=left_cols.at[:, pl.ds(pl.multiple_of(source * 16, 16), 16), :],
                send_sem=left_send.at[0],
                recv_sem=left_recv.at[source],
                device_id=sibling,
                device_id_type=MESH,
            ).wait_recv()

        vir_cols = jnp.transpose(jnp.broadcast_to(vir_ref[:, my_lanes], (LANES, LANES)))[:, :1]
        shifts = []
        for pair in range(pairs):
            left_rows[pl.ds(pair * LANES, LANES), :] = jnp.transpose(left_cols[pair])
            shifts.append((occ_ref[left_ref[pair]] + occ_ref[second]) - vir_cols)
        wide = 4 * LANES

        def work(low, high):
            shift = jnp.concatenate(shifts[low:high], axis=0)
            left = left_rows[pl.ds(low * LANES, (high - low) * LANES), :]
            total = jnp.zeros(left.shape, jnp.float32)
            for part in range(virtuals // wide):
                columns = pl.ds(part * wide, wide)
                if low == 0:
                    side, first = divmod(part * wide, half)
                    block = full[:, pl.ds(8 * side, 8), pl.ds(first, wide)].astype(jnp.float32)
                    plain[:, columns] = block.reshape(plain.shape[0], wide).astype(jnp.bfloat16)
                block = plain[:, columns]
                integral = jnp.dot(left, block, preferred_element_type=jnp.float32)
                denominator = shift - vir_ref[:, columns]
                inverse = pl.reciprocal(denominator, approx=True)
                inverse = inverse * (2.0 - denominator * inverse)
                amplitude = (integral * inverse).astype(jnp.bfloat16)
                total += lax.dot_general(
                    amplitude, block, (((1,), (1,)), ((), ())), preferred_element_type=jnp.float32
                )
            for pair in range(low, high):
                first = (pair - low) * LANES
                contrib[pair] = jnp.transpose(total[first : first + LANES])
                out_ref[pair, :, my_lanes] = contrib[pair, pl.ds(pl.multiple_of(me * 8, 8), 8), :]
            for_out(lambda copy: copy.start(), low, high)

        work(0, 1)
        work(1, pairs)

    swap.wait_send()
    for copy in started:
        copy.wait_send()

    for_left(lambda copy: copy.wait_send())
    mine = jnp.where(inner == idle, -1, my_tile)

    @pl.loop(0, tiles)
    def _(tile):
        @pl.when(tile != mine)
        def _():
            pltpu.make_async_remote_copy(
                src_ref=contrib.at[:, pl.ds(0, 8), :],
                dst_ref=out_ref.at[:, :, pl.ds(pl.multiple_of(tile * LANES, LANES), LANES)],
                send_sem=out_send.at[0],
                recv_sem=out_recv.at[tile],
                device_id=sibling,
                device_id_type=MESH,
            ).wait_recv()

    @pl.when(inner != idle)
    def _():
        for_out(lambda copy: copy.wait_send())


def add_pairs(left_ref, returned_ref, gamma_ref, rows, sems):
    copies = []
    for orbital in range(rows.shape[0]):
        row = jnp.where(left_ref[0] == orbital, returned_ref[0], 0.0)
        for pair in range(1, returned_ref.shape[0]):
            row += jnp.where(left_ref[pair] == orbital, returned_ref[pair], 0.0)
        rows[orbital] = row
        copies.append(pltpu.make_async_copy(rows.at[orbital], gamma_ref.at[orbital], sems.at[orbital]))
        copies[-1].start()
    for copy in copies:
        copy.wait()


def body_tiles(b_tensor, occ_energy, vir_energy, left_list, right_occ):
    occ_count, aux_rows, virtuals = b_tensor.shape
    pairs = left_list.shape[0]
    aux = 32 * aux_rows
    hbm, vmem = pl.BlockSpec(memory_space=pltpu.HBM), pl.BlockSpec(memory_space=pltpu.VMEM)
    dma = pltpu.SemaphoreType.DMA
    returned = pl.pallas_call(
        kernel,
        out_shape=jax.ShapeDtypeStruct((pairs, aux_rows, virtuals), jnp.float32),
        in_specs=[hbm] * 5,
        out_specs=vmem,
        scratch_shapes=[
            pltpu.VMEM(b_tensor.shape, jnp.bfloat16),
            pltpu.SMEM(occ_energy.shape, jnp.float32),
            pltpu.VMEM((1, virtuals), jnp.float32),
            pltpu.SMEM(left_list.shape, jnp.int32),
            pltpu.SMEM(right_occ.shape, jnp.int32),
            dma((5,)),
            pltpu.VMEM(((pairs + 1) * aux_rows, virtuals), jnp.bfloat16),
            pltpu.VMEM(((pairs + 1) * aux_rows, virtuals), jnp.bfloat16),
            pltpu.VMEM((2 * aux_rows, virtuals // 2), jnp.bfloat16),
            pltpu.VMEM((pairs, 2 * aux_rows, virtuals), jnp.bfloat16),
            pltpu.VMEM((32, 2 * aux_rows, virtuals // 2), jnp.bfloat16),
            pltpu.VMEM((pairs, aux, LANES), jnp.bfloat16),
            pltpu.VMEM((pairs * LANES, aux), jnp.bfloat16),
            pltpu.VMEM((aux, virtuals), jnp.bfloat16),
            pltpu.VMEM((pairs, aux, LANES), jnp.float32),
            dma, dma, dma((32,)), dma((32,)), dma((virtuals // LANES,)), dma((16,)),
            dma((32,)), dma((virtuals // LANES,)),
        ],
        compiler_params=pltpu.CompilerParams(
            collective_id=0, has_side_effects=True, vmem_limit_bytes=60 * 2**20
        ),
        cost_estimate=pl.CostEstimate(
            flops=4 * pairs * aux * virtuals * LANES, bytes_accessed=2 * occ_count * aux_rows * virtuals, transcendentals=0
        ),
    )(b_tensor, occ_energy, vir_energy.reshape(1, virtuals), left_list, right_occ)
    return pl.pallas_call(
        add_pairs,
        out_shape=jax.ShapeDtypeStruct(b_tensor.shape, jnp.float32),
        in_specs=[pl.BlockSpec(memory_space=pltpu.SMEM), vmem],
        out_specs=hbm,
        scratch_shapes=[pltpu.VMEM(b_tensor.shape, jnp.float32), dma((occ_count,))],
    )(left_list, returned)


def solution(mesh):
    placed = (P(None, ("grp", "inner"), None), P(), P(), P(), P())
    plan = body
    if mesh.shape["grp"] == 8 and mesh.shape["inner"] == 4:
        plan = body_tiles

    def program(b_tensor, *rest):
        aux, virtuals = b_tensor.shape[1:]
        fits = aux == 256 and virtuals == 3072
        return jax.shard_map(
            plan if fits else body,
            mesh=mesh,
            in_specs=placed,
            out_specs=P(None, ("grp", "inner"), None),
            check_vma=False,
        )(b_tensor, *rest)

    return program
```
